32 devices in a mesh: orow: 8 (over z, x), ocol: 4 (over y, core).
Axes of the slice: x: 2, y: 2, z: 4, core: 2. Of those that a mesh axis runs over, the one named last changes fastest.
Arguments:
- amplitudes: bfloat16 [16, 16, 512, 512], P('orow', 'ocol'), may hold values from -6 to 6
- tile_mask: int32 [16, 16, 2, 2], P('orow', 'ocol'), may hold values 0 or 1
- domain_tiles: int32 [16, 16, 2], replicated, may hold values from 0 to 7, as said below
- cholesky: bfloat16 [4, 2048, 2048], P('ocol'), as said below
Outputs:
- ladder_sym: float32 [16, 16, 512, 512], P('orow', 'ocol')
The draws below stay inside these ranges and needn't reach their ends.
Inputs may be any that keep to these rules, and one draw needn't show every extreme that they name: `domain_tiles`: for every pair the 2 tile numbers differ, and pair (j, i) lists the same tiles in the same order as pair (i, j). Every vector cholesky[q] is a symmetric 2048 x 2048 matrix.
All inputs are finite; a program needn't handle non-finite values. No bound on the sum of `tile_mask` on one device may be relied on, other than what follows from the above.
Results may differ from the reference program's by a relative error of at most 0.0029.
Values may be sent and summed in bfloat16 or wider, within the bound.
No kernel may reach another device: no remote copies, remote signals or barrier semaphores. Data moves between devices by JAX's collectives and lax.ppermute only.
A program may use at most 128 MiB of HBM per device.

```python
import jax
import jax.numpy as jnp
from jax import lax

TILE = 256
NT = 8
K = 2
NO = 16
NQ = 4
V = 2048
DV = 512


def draw_domain_tiles(key, part):
    first_key, second_key = jax.random.split(jax.random.fold_in(key, 7))
    first = jax.random.randint(first_key, (NO, NO), 0, NT)
    offset = jax.random.randint(second_key, (NO, NO), 1, NT)
    second = (first + offset) % NT
    both = jnp.stack([first, second], axis=-1).astype(jnp.int32)
    rows = jnp.arange(NO, dtype=jnp.int32)[:, None, None]
    cols = jnp.arange(NO, dtype=jnp.int32)[None, :, None]
    return jnp.where(rows <= cols, both, both.transpose(1, 0, 2)).astype(jnp.int32)


def draw_cholesky(key, part):
    sub_key = jax.random.fold_in(key, 11)
    spread = (2.0 / (4.0 * DV)) ** 0.5
    raw = jnp.clip(jax.random.normal(sub_key, (NQ, V, V), jnp.float32), -6.0, 6.0)
    mirrored = (raw + raw.transpose(0, 2, 1)) * (0.5 * spread)
    return mirrored.astype(jnp.bfloat16)


def place_ends(entries, stream_key, least, high):
    place = [jax.random.randint(jax.random.fold_in(stream_key, axis), (), 0, length) for axis, length in enumerate(entries.shape)]
    main_axis = entries.shape.index(max(entries.shape))
    neighbour = place[:main_axis] + [(place[main_axis] + 1) % entries.shape[main_axis]] + place[main_axis + 1:]
    return entries.at[tuple(place)].set(least).at[tuple(neighbour)].set(high)


def level_of(stream_key, extent, cuts, low, top_value):
    loudness, own = 1.0, jax.random.fold_in(stream_key, 6)
    for dim, shards_of in cuts:
        heights = jnp.exp(jax.random.uniform(jax.random.fold_in(own, dim), (shards_of,), jnp.float32, low / len(cuts), top_value / len(cuts)))
        loudness = loudness * jnp.repeat(heights, extent[dim] // shards_of).reshape([-1 if axis == dim else 1 for axis in range(len(extent))])
    return loudness


def bell_draw(key, extent, scale, limit, shards=(), kind=jnp.bfloat16):
    factor_of = level_of(key, extent, shards, -0.22, 0.18) if shards else 1.0
    array = jax.random.normal(key, extent, jnp.float32) * scale * factor_of
    return jnp.minimum(jnp.maximum(array, -limit), limit).astype(kind)


def setup_inputs(seed: int = 0) -> dict:
    key_list = jax.random.split(jax.random.key(seed), 5)
    return {
        "amplitudes": bell_draw(key_list[0], (NO, NO, DV, DV), 1.0, 6.0, ((0, 8), (1, 4))),
        "tile_mask": place_ends((jax.random.randint(key_list[1], (NO, NO, K, K), 0, 4) < 3).astype(jnp.int32), jax.random.fold_in(key_list[1], 1), 0, 1),
        "domain_tiles": draw_domain_tiles(jax.random.fold_in(key_list[4], 71), 0),
        "cholesky": draw_cholesky(jax.random.fold_in(key_list[4], 71), 0),
    }


def pick_tiles(factor_all, chosen):
    number = factor_all.shape[0]
    tiles = factor_all.shape[1] // TILE
    blocked = factor_all.reshape(number, tiles, TILE, tiles, TILE)
    picked = blocked[:, chosen[:, None], :, chosen[None, :], :]
    width = chosen.shape[0] * TILE
    return picked.transpose(2, 0, 3, 1, 4).reshape(number, width, width)


def reference(amplitudes, tile_mask, domain_tiles, cholesky):
    def one_pair(flat_index):
        row_index = flat_index // NO
        col_index = flat_index % NO
        sub_factor = pick_tiles(cholesky, domain_tiles[row_index, col_index])
        shaped = amplitudes[row_index, col_index].reshape(K, TILE, K, TILE)
        weights = tile_mask[row_index, col_index].astype(jnp.bfloat16)[:, None, :, None]
        weighted = (shaped * weights).reshape(K * TILE, K * TILE)
        inner = jnp.einsum("qac,cd->qad", sub_factor.astype(jnp.float32), weighted.astype(jnp.float32)).astype(jnp.bfloat16)
        return jnp.einsum("qad,qbd->ab", inner.astype(jnp.float32), sub_factor.astype(jnp.float32))

    flat = lax.map(one_pair, jnp.arange(NO * NO, dtype=jnp.int32))
    ladder = flat.reshape(NO, NO, K * TILE, K * TILE)
    return ladder + ladder.transpose(1, 0, 3, 2)
```

```python
import functools

import jax
import jax.numpy as jnp
from jax import lax
from jax.experimental import pallas as pl
from jax.experimental.pallas import tpu as pltpu
from jax.sharding import PartitionSpec as P

AXES = ("orow", "ocol")


def pack_kernel(count, width, place_ref, source_ref, packed_ref, sems):
    copies = []
    for n in range(count):
        row = pl.multiple_of(place_ref[3 * n + 1] * width, width)
        col = pl.multiple_of(place_ref[3 * n + 2] * width, width)
        copies.append(
            pltpu.make_async_copy(
                source_ref.at[place_ref[3 * n], pl.ds(row, width), pl.ds(col, width)],
                packed_ref.at[n],
                sems.at[n],
            )
        )
    for copy in copies:
        copy.start()
    for copy in copies:
        copy.wait()


def pack_tiles(cholesky, places, width):
    count = places.shape[0]
    size = count * width * width * cholesky.dtype.itemsize
    return pl.pallas_call(
        functools.partial(pack_kernel, count, width),
        out_shape=jax.ShapeDtypeStruct((count, width, width), cholesky.dtype),
        grid_spec=pltpu.PrefetchScalarGridSpec(
            num_scalar_prefetch=1,
            grid=(1,),
            in_specs=[pl.BlockSpec(memory_space=pl.ANY)],
            out_specs=pl.BlockSpec(memory_space=pl.ANY),
            scratch_shapes=[pltpu.SemaphoreType.DMA((count,))],
        ),
        cost_estimate=pl.CostEstimate(flops=0, bytes_accessed=2 * size, transcendentals=0),
        name="pack_tiles",
    )(places.reshape(-1), cholesky)


def ladder_kernel(depth, tiles, width, number, pairs, vectors, *refs):
    bank_ref, place_ref, flip_ref, own_ref, mask_ref = refs[:5]
    amps_ref, partner_ref = refs[5:7]
    banks = refs[7 : 7 + number]
    out_ref, factor, weighted, sems = refs[-4:]
    pair, vector = pl.program_id(0), pl.program_id(1)
    step = pair * vectors + vector
    slots = [(a, b) for a in range(tiles) for b in range(a, tiles)]

    def corner(index):
        return pl.ds(pl.multiple_of(index * width, width), width)

    def target(which, at, slot):
        a, b = slots[which]
        if a == b:
            return factor.at[slot, corner(a), corner(b)]
        flip = flip_ref[at * len(slots) + which]
        return factor.at[slot, corner(a + flip * (b - a)), corner(b + flip * (a - b))]

    def fetch(which, at_step, slot):
        entry = at_step * len(slots) + which
        for n, bank in enumerate(banks):
            @pl.when(bank_ref[entry] == n)
            def _():
                pltpu.make_async_copy(
                    bank.at[place_ref[entry]],
                    target(which, at_step // vectors, slot),
                    sems.at[slot, which],
                ).start()

    slot = lax.rem(step, 2)

    @pl.when(step == 0)
    def _():
        for which in range(len(slots)):
            fetch(which, step, slot)

    @pl.when(step + 1 < pairs * vectors)
    def _():
        for which in range(len(slots)):
            fetch(which, step + 1, 1 - slot)

    @pl.when(vector == 0)
    def _():
        for a in range(tiles):
            for b in range(tiles):
                keep = mask_ref[(pair * tiles + a) * tiles + b].astype(jnp.float32)
                block = amps_ref[0, 0, a * width : (a + 1) * width, b * width : (b + 1) * width]
                weighted[a * width : (a + 1) * width, b * width : (b + 1) * width] = (
                    block.astype(jnp.float32) * keep
                ).astype(block.dtype)

    for which, (a, b) in enumerate(slots):
        pltpu.make_async_copy(
            banks[0].at[0], target(which, pair, slot), sems.at[slot, which]
        ).wait()
    for which, (a, b) in enumerate(slots):
        if a != b:
            flip = flip_ref[pair * len(slots) + which]
            row, col = a + flip * (b - a), b + flip * (a - b)
            factor[slot, corner(col), corner(row)] = factor[slot, corner(row), corner(col)].T

    whole = factor[slot]
    inner = jnp.dot(whole, weighted[...], preferred_element_type=jnp.float32)
    inner += lax.dot_general(
        whole, partner_ref[0, 0], (((1,), (1,)), ((), ())), preferred_element_type=jnp.float32
    )
    term = jnp.dot(inner.astype(jnp.bfloat16), whole, preferred_element_type=jnp.float32)

    @pl.when(vector == 0)
    def _():
        out_ref[0, 0] = term

    @pl.when(vector > 0)
    def _():
        out_ref[0, 0] += term


def ladder_part(amplitudes, partner, banks, tables, total, vectors):
    bank, place, flip, own, mask = tables
    pairs = own.shape[0]
    tiles = mask.shape[-1]
    depth = amplitudes.shape[-1]
    width = depth // tiles
    slots = tiles * (tiles + 1) // 2
    partner_cols = partner.shape[1]
    rows = partner.shape[0]

    def own_map(pair, vector, bank, place, flip, own, mask):
        return own[2 * pair], own[2 * pair + 1], 0, 0

    def partner_map(pair, vector, *_):
        return lax.rem(pair, rows), pair // rows, 0, 0

    block = (1, 1, depth, depth)
    in_specs = [pl.BlockSpec(block, own_map), pl.BlockSpec(block, partner_map)]
    in_specs += [pl.BlockSpec(memory_space=pl.ANY)] * len(banks)
    operands = [amplitudes, partner, *banks]
    aliases = {}
    if total is not None:
        aliases = {5 + len(operands): 0}
        operands.append(total)
        in_specs.append(pl.BlockSpec(memory_space=pl.ANY))
    flops = 6 * pairs * vectors * depth**3
    moved = pairs * (depth * depth * 8 + vectors * slots * width * width * 2)
    return pl.pallas_call(
        functools.partial(ladder_kernel, depth, tiles, width, len(banks), pairs, vectors),
        out_shape=jax.ShapeDtypeStruct(amplitudes.shape, jnp.float32),
        grid_spec=pltpu.PrefetchScalarGridSpec(
            num_scalar_prefetch=5,
            grid=(pairs, vectors),
            in_specs=in_specs,
            out_specs=pl.BlockSpec(block, own_map),
            scratch_shapes=[
                pltpu.VMEM((2, depth, depth), jnp.bfloat16),
                pltpu.VMEM((depth, depth), jnp.bfloat16),
                pltpu.SemaphoreType.DMA((2, slots)),
            ],
        ),
        input_output_aliases=aliases,
        compiler_params=pltpu.CompilerParams(
            dimension_semantics=("arbitrary", "arbitrary"), vmem_limit_bytes=32 * 2**20
        ),
        cost_estimate=pl.CostEstimate(flops=flops, bytes_accessed=moved, transcendentals=0),
        name="ladder_part",
    )(
        bank.reshape(-1), place.reshape(-1), flip.reshape(-1), own.reshape(-1), mask.reshape(-1),
        *operands,
    )


def swapped(rows, cols, change):
    return [
        (r * cols + c, change(r, c)[0] * cols + change(r, c)[1])
        for r in range(rows)
        for c in range(cols)
    ]


def shards(rows, cols, amplitudes, tile_mask, domain_tiles, cholesky):
    row_pairs, col_pairs, depth, _ = amplitudes.shape
    tiles = domain_tiles.shape[-1]
    width = depth // tiles
    held = cholesky.shape[0]
    across = cholesky.shape[1] // width
    vectors = held * cols
    ratio = col_pairs // row_pairs
    r, c = lax.axis_index("orow"), lax.axis_index("ocol")

    upper = [(s, t) for s in range(across) for t in range(s, across)]
    half = (len(upper) + 1) // 2
    padded = upper + upper[: 2 * half - len(upper)]
    number_of = [[0] * across for _ in range(across)]
    for n, (s, t) in enumerate(upper):
        number_of[s][t] = number_of[t][s] = n
    number_of = jnp.asarray(number_of, jnp.int32)
    places = jnp.asarray(
        [[[q, s, t] for q in range(held) for s, t in padded[k * half : (k + 1) * half]] for k in range(2)],
        jnp.int32,
    )

    weighted = []
    for k in range(ratio):
        start = lax.rem(r + k, ratio) * row_pairs
        piece = lax.dynamic_slice_in_dim(amplitudes, start, row_pairs, 1)
        keep = lax.dynamic_slice_in_dim(tile_mask, start, row_pairs, 1)
        shaped = piece.reshape(row_pairs, row_pairs, tiles, width, tiles, width)
        shaped = shaped * keep.astype(piece.dtype)[:, :, :, None, :, None]
        weighted.append(shaped.reshape(piece.shape))
    partners = [
        lax.ppermute(
            piece, AXES,
            swapped(rows, cols, lambda a, b: (ratio * b + (a + k) % ratio, a // ratio)),
        )
        for k, piece in enumerate(weighted)
    ]

    side = lax.rem(r, 2)
    if cols == 4 and rows % 2 == 0:
        mine = pack_tiles(cholesky, places[side], width)
        rest = pack_tiles(cholesky, places[1 - side], width)
        over_y = swapped(rows, cols, lambda a, b: (a, b ^ 2))
        over_x = swapped(rows, cols, lambda a, b: (a ^ 1, b))
        over_core = swapped(rows, cols, lambda a, b: (a, b ^ 1))
        far = lax.ppermute(mine, AXES, over_y)
        far_rest = lax.ppermute(far, AXES, over_x)
        banks = [
            mine, rest,
            lax.ppermute(mine, AXES, over_core), lax.ppermute(rest, AXES, over_core),
            far, far_rest,
            lax.ppermute(far, AXES, over_core), lax.ppermute(far_rest, AXES, over_core),
        ]

        def locate(vector, number):
            slot = vector // held
            bank = 2 * slot + jnp.where(number // half == side, 0, 1)
            return bank, lax.rem(vector, held) * half + lax.rem(number, half)
    else:
        whole = jnp.concatenate([places[0], places[1]], axis=0)
        packed = pack_tiles(cholesky, whole, width)
        banks = [lax.all_gather(packed, "ocol", axis=0, tiled=True)]

        def locate(vector, number):
            inside = (number // half) * (held * half) + lax.rem(vector, held) * half + lax.rem(number, half)
            return jnp.zeros_like(inside), (vector // held) * (2 * held * half) + inside

    domains = lax.dynamic_slice(
        domain_tiles, (r * row_pairs, c * col_pairs, 0), (row_pairs, col_pairs, tiles)
    )
    slots = [(a, b) for a in range(tiles) for b in range(a, tiles)]
    total = None
    for k in range(ratio):
        block = lax.rem(r + ratio - k, ratio)
        pair = jnp.arange(row_pairs * row_pairs, dtype=jnp.int32)
        own_row = pair // row_pairs
        own_col = block * row_pairs + lax.rem(pair, row_pairs)
        chosen = domains[own_row, own_col]
        first = jnp.stack([chosen[:, a] for a, _ in slots], axis=-1)
        second = jnp.stack([chosen[:, b] for _, b in slots], axis=-1)
        flip = (first > second).astype(jnp.int32)
        number = number_of[first, second][:, None, :]
        vector = jnp.arange(vectors, dtype=jnp.int32)[None, :, None]
        bank, place = locate(vector, number)
        bank, place = jnp.broadcast_arrays(bank, place)
        own = jnp.stack([own_row, own_col], axis=-1)
        mask = tile_mask[own_row, own_col]
        total = ladder_part(
            amplitudes, partners[k], banks, (bank, place, flip, own, mask), total, vectors
        )
    return total


def solution(mesh):
    return jax.shard_map(
        functools.partial(shards, mesh.shape["orow"], mesh.shape["ocol"]),
        mesh=mesh,
        in_specs=(
            P("orow", "ocol", None, None),
            P("orow", "ocol", None, None),
            P(),
            P("ocol", None, None),
        ),
        out_specs=P("orow", "ocol", None, None),
        check_vma=False,
    )
```

```python
import functools

import jax
import jax.numpy as jnp
from jax import lax
from jax.experimental import pallas as pl
from jax.experimental.pallas import tpu as pltpu
from jax.sharding import PartitionSpec as P

AXES = ("orow", "ocol")
ANY = pl.BlockSpec(memory_space=pl.ANY)
VMEM = 56 * 2**20


def pack_kernel(sizes, width, place_ref, source_ref, *refs):
    held, sems = refs[-2:]
    packed = refs[-2 - len(sizes) : -2]
    loads, stores = [], []
    for part, size in enumerate(sizes):
        for inside in range(size):
            n = len(loads)
            row = pl.multiple_of(place_ref[3 * n + 1] * width, width)
            col = pl.multiple_of(place_ref[3 * n + 2] * width, width)
            loads.append(
                pltpu.make_async_copy(
                    source_ref.at[place_ref[3 * n], pl.ds(row, width), pl.ds(col, width)],
                    held.at[n],
                    sems.at[0, n],
                )
            )
            stores.append(pltpu.make_async_copy(held.at[n], packed[part].at[inside], sems.at[1, n]))
    for load in loads:
        load.start()
    for load, store in zip(loads, stores):
        load.wait()
        store.start()
    for store in stores:
        store.wait()


def pick_kernel(sizes, place_ref, first_ref, second_ref, *refs):
    held, sems = refs[-2:]
    packed = refs[-2 - len(sizes) : -2]
    stores = []
    for part, size in enumerate(sizes):
        for inside in range(size):
            n = len(stores)
            for m, source in enumerate((first_ref, second_ref)):
                @pl.when(place_ref[2 * n] == m)
                def _():
                    pltpu.make_async_copy(
                        source.at[place_ref[2 * n + 1]], held.at[n], sems.at[0, n]
                    ).start()
            stores.append(pltpu.make_async_copy(held.at[n], packed[part].at[inside], sems.at[1, n]))
    for n, store in enumerate(stores):
        pltpu.make_async_copy(first_ref.at[0], held.at[n], sems.at[0, n]).wait()
        store.start()
    for store in stores:
        store.wait()


def pack(kernel, places, sources, width, sizes, after=()):
    count, dtype = sum(sizes), sources[0].dtype
    return pl.pallas_call(
        kernel,
        out_shape=[jax.ShapeDtypeStruct((size, width, width), dtype) for size in sizes],
        grid_spec=pltpu.PrefetchScalarGridSpec(
            num_scalar_prefetch=1,
            grid=(1,),
            in_specs=[ANY] * (len(sources) + len(after)),
            out_specs=[ANY] * len(sizes),
            scratch_shapes=[
                pltpu.VMEM((count, width, width), dtype),
                pltpu.SemaphoreType.DMA((2, count)),
            ],
        ),
        compiler_params=pltpu.CompilerParams(vmem_limit_bytes=VMEM),
        cost_estimate=pl.CostEstimate(
            flops=0, bytes_accessed=count * width * width // 16, transcendentals=0
        ),
        name="pack_tiles",
    )(places.reshape(-1), *sources, *after)


def keep_tiles(source, mask_ref, base, tiles, width, store):
    for a in range(tiles):
        for b in range(tiles):
            rows, cols = slice(a * width, (a + 1) * width), slice(b * width, (b + 1) * width)
            block = source[rows, cols]
            store(rows, cols, block * mask_ref[base + a * tiles + b].astype(block.dtype))


def send_kernel(tiles, width, rows, col_pairs, first, *refs):
    start_ref, mask_ref, amps_ref = refs[:3]
    out_ref = refs[-1]
    pair = first + pl.program_id(0)
    base = ((pair // rows) * col_pairs + start_ref[0] + lax.rem(pair, rows)) * tiles * tiles

    def store(rows, cols, value):
        out_ref[0, rows, cols] = value

    keep_tiles(amps_ref.at[0, 0], mask_ref, base, tiles, width, store)


def sent_pairs(amplitudes, tile_mask, col, first, count, after=()):
    rows, col_pairs, depth, _ = amplitudes.shape
    tiles = tile_mask.shape[-1]

    def source(i, start, mask):
        return (first + i) // rows, start[0] + lax.rem(first + i, rows), 0, 0

    return pl.pallas_call(
        functools.partial(send_kernel, tiles, depth // tiles, rows, col_pairs, first),
        out_shape=jax.ShapeDtypeStruct((count, depth, depth), amplitudes.dtype),
        grid_spec=pltpu.PrefetchScalarGridSpec(
            num_scalar_prefetch=2,
            grid=(count,),
            in_specs=[pl.BlockSpec((1, 1, depth, depth), source)] + [ANY] * len(after),
            out_specs=pl.BlockSpec((1, depth, depth), lambda i, start, mask: (i, 0, 0)),
        ),
        compiler_params=pltpu.CompilerParams(vmem_limit_bytes=VMEM),
        cost_estimate=pl.CostEstimate(
            flops=0, bytes_accessed=count * depth * depth // 16, transcendentals=0
        ),
        name="sent_pairs",
    )(col.reshape(1).astype(jnp.int32), tile_mask.reshape(-1), amplitudes, *after)


def ladder_kernel(tiles, width, counts, number, vectors, adds, col_pairs, *refs):
    bank_ref, place_ref, flip_ref, own_ref, mask_ref = refs[:5]
    amps_ref = refs[5]
    pieces, at = [], 6
    for arrays, pairs in counts:
        pieces.append((refs[at : at + arrays], pairs))
        at += arrays
    banks = refs[at : at + number]
    total_ref = refs[at + number] if adds else None
    out_ref, factor, weighted, partner, sems = refs[-5:]
    pair, steps = pl.program_id(0), pl.num_programs(0)
    slots = [(a, b) for a in range(tiles) for b in range(a, tiles)]

    def corner(index):
        return pl.ds(pl.multiple_of(index * width, width), width)

    def ends(which, pair):
        a, b = slots[which]
        if a == b:
            return a, b
        flip = flip_ref[pair * len(slots) + which]
        return a + flip * (b - a), b + flip * (a - b)

    def fetch(pair, slot):
        for vector in range(vectors):
            for which in range(len(slots)):
                entry = (pair * vectors + vector) * len(slots) + which
                row, col = ends(which, pair)
                for n, bank in enumerate(banks):
                    @pl.when(bank_ref[entry] == n)
                    def _():
                        pltpu.make_async_copy(
                            bank.at[place_ref[entry]],
                            factor.at[slot, vector, corner(row), corner(col)],
                            sems.at[slot, vector, which],
                        ).start()

    slot = lax.rem(pair, 2)

    @pl.when(pair == 0)
    def _():
        fetch(pair, slot)

    @pl.when(pair + 1 < steps)
    def _():
        fetch(pair + 1, 1 - slot)

    def store(rows, cols, value):
        weighted[rows, cols] = value

    base = (own_ref[2 * pair] * col_pairs + own_ref[2 * pair + 1]) * tiles * tiles
    keep_tiles(amps_ref.at[0, 0], mask_ref, base, tiles, width, store)
    first = 0
    for arrays, pairs in pieces:
        @pl.when((pair >= first) & (pair < first + pairs))
        def _():
            value = arrays[0][0]
            for other in arrays[1:]:
                value += other[0]
            partner[...] = value
        first += pairs

    for vector in range(vectors):
        for which in range(len(slots)):
            row, col = ends(which, pair)
            pltpu.make_async_copy(
                banks[0].at[0],
                factor.at[slot, vector, corner(row), corner(col)],
                sems.at[slot, vector, which],
            ).wait()
            if slots[which][0] != slots[which][1]:
                factor[slot, vector, corner(col), corner(row)] = factor[
                    slot, vector, corner(row), corner(col)
                ].T

    total = total_ref[0, 0] if adds else None
    for vector in range(vectors):
        whole = factor[slot, vector]
        inner = jnp.dot(whole, weighted[...], preferred_element_type=jnp.float32)
        inner += lax.dot_general(
            whole, partner[...], (((1,), (1,)), ((), ())), preferred_element_type=jnp.float32
        )
        term = jnp.dot(inner.astype(jnp.bfloat16), whole, preferred_element_type=jnp.float32)
        total = term if total is None else total + term
    out_ref[0, 0] = total


def ladder_part(amplitudes, tile_mask, pieces, banks, tables, total, adds):
    bank, place, flip, own = tables
    pairs, vectors, slots = bank.shape
    tiles = tile_mask.shape[-1]
    col_pairs, depth = amplitudes.shape[1:3]
    width = depth // tiles
    block = (1, 1, depth, depth)

    def own_map(pair, bank, place, flip, own, mask):
        return own[2 * pair], own[2 * pair + 1], 0, 0

    def piece_map(first, count):
        return lambda pair, *_: (jnp.clip(pair - first, 0, count - 1), 0, 0)

    in_specs, operands, counts, first = [pl.BlockSpec(block, own_map)], [amplitudes], [], 0
    for arrays in pieces:
        count = arrays[0].shape[0]
        for array in arrays:
            in_specs.append(pl.BlockSpec((1, depth, depth), piece_map(first, count)))
            operands.append(array)
        counts.append((len(arrays), count))
        first += count
    in_specs += [ANY] * len(banks)
    operands += banks
    aliases = {}
    if total is not None:
        aliases = {5 + len(operands): 0}
        operands.append(total)
        in_specs.append(pl.BlockSpec(block, own_map) if adds else ANY)
    flops = 6 * pairs * vectors * depth**3
    moved = pairs * (depth * depth * 8 + vectors * slots * width * width * 2)
    return pl.pallas_call(
        functools.partial(
            ladder_kernel, tiles, width, tuple(counts), len(banks), vectors, adds, col_pairs
        ),
        out_shape=jax.ShapeDtypeStruct(amplitudes.shape, jnp.float32),
        grid_spec=pltpu.PrefetchScalarGridSpec(
            num_scalar_prefetch=5,
            grid=(pairs,),
            in_specs=in_specs,
            out_specs=pl.BlockSpec(block, own_map),
            scratch_shapes=[
                pltpu.VMEM((2, vectors, depth, depth), jnp.bfloat16),
                pltpu.VMEM((depth, depth), jnp.bfloat16),
                pltpu.VMEM((depth, depth), jnp.bfloat16),
                pltpu.SemaphoreType.DMA((2, vectors, slots)),
            ],
        ),
        input_output_aliases=aliases,
        compiler_params=pltpu.CompilerParams(
            dimension_semantics=("arbitrary",), vmem_limit_bytes=VMEM
        ),
        cost_estimate=pl.CostEstimate(flops=flops // 64, bytes_accessed=moved // 64, transcendentals=0),
        name="ladder_part",
    )(
        bank.reshape(-1), place.reshape(-1), flip.reshape(-1), own.reshape(-1),
        tile_mask.reshape(-1), *operands,
    )


def gate_kernel(*refs):
    pass


def gate(values, after):
    return pl.pallas_call(
        gate_kernel,
        out_shape=[jax.ShapeDtypeStruct(value.shape, value.dtype) for value in values],
        in_specs=[ANY] * (len(values) + len(after)),
        out_specs=[ANY] * len(values),
        input_output_aliases={n: n for n in range(len(values))},
        compiler_params=pltpu.CompilerParams(vmem_limit_bytes=VMEM),
        cost_estimate=pl.CostEstimate(flops=0, bytes_accessed=0, transcendentals=0),
        name="gate",
    )(*values, *after)


def moves(rows, cols, change, chosen=lambda r, c: True):
    pairs = []
    for r in range(rows):
        for c in range(cols):
            if chosen(r, c):
                to_row, to_col = change(r, c)
                pairs.append((r * cols + c, to_row * cols + to_col))
    return pairs


def shards(rows, cols, amplitudes, tile_mask, domain_tiles, cholesky):
    row_pairs, col_pairs, depth, _ = amplitudes.shape
    tiles = domain_tiles.shape[-1]
    width = depth // tiles
    held = cholesky.shape[0]
    across = cholesky.shape[1] // width
    vectors = held * cols
    ratio = col_pairs // row_pairs
    r, c = lax.axis_index("orow"), lax.axis_index("ocol")

    paths = rows == 8 and cols == 4 and row_pairs == 2 and held == 1

    upper = [(s, t) for s in range(across) for t in range(s, across)]
    places = jnp.asarray([[q, s, t] for q in range(held) for s, t in upper], jnp.int32)
    quarter = -(-len(upper) // 4)
    cut = -(-2 * quarter // 3)

    pair = jnp.arange(row_pairs * col_pairs, dtype=jnp.int32)
    turn = pair // (row_pairs * row_pairs)
    own_row = lax.rem(pair, row_pairs)
    own_col = lax.rem(r + ratio - turn, ratio) * row_pairs + lax.rem(pair // row_pairs, row_pairs)
    chosen = domain_tiles[r * row_pairs + own_row, c * col_pairs + own_col]
    corners = [(a, b) for a in range(tiles) for b in range(a, tiles)]
    first = jnp.stack([chosen[:, a] for a, _ in corners], axis=-1)
    second = jnp.stack([chosen[:, b] for _, b in corners], axis=-1)
    flip = (first > second).astype(jnp.int32)
    low, high = jnp.minimum(first, second), jnp.maximum(first, second)
    number = (low * across - low * (low - 1) // 2 + high - low)[:, None, :]
    vector = jnp.arange(vectors, dtype=jnp.int32)[None, :, None]
    own = jnp.stack([own_row, own_col], axis=-1)
    side = lax.rem(r, 2)

    def target(turn):
        return lambda a, b: (ratio * b + (a + turn) % ratio, a // ratio)

    def sent(turn, first, count, after=()):
        col = lax.rem(r + turn, ratio) * row_pairs
        return sent_pairs(amplitudes, tile_mask, col, first, count, after)

    def tables(bank, place, which, chosen_vectors):
        return (
            jnp.concatenate([bank[w, chosen_vectors] for w in which]),
            jnp.concatenate([place[w, chosen_vectors] for w in which]),
            jnp.concatenate([flip[w] for w in which]),
            jnp.concatenate([own[w] for w in which]),
        )

    pack_near = lambda after=(): pack(
        functools.partial(pack_kernel, (len(places),), width), places, [cholesky], width,
        (len(places),), after,
    )[0]

    if not paths:
        banks = [lax.all_gather(pack_near(), "ocol", axis=0, tiled=True)]
        place = vector * len(upper) + number
        bank = jnp.zeros_like(place)
        pieces = [
            (lax.ppermute(sent(turn, 0, row_pairs * row_pairs), AXES, moves(rows, cols, target(turn))),)
            for turn in range(ratio)
        ]
        every = tables(bank, place, [slice(None)], slice(None))
        return ladder_part(amplitudes, tile_mask, pieces, banks, every, None, False)

    crosses = lambda a, b: (a // 4) != (b // 2)
    stays = lambda a, b: not crosses(a, b)
    over_y = moves(rows, cols, lambda a, b: (a, b ^ 2))
    over_x = moves(rows, cols, lambda a, b: (a ^ 1, b))
    over_core = moves(rows, cols, lambda a, b: (a, b ^ 1))
    hop = moves(rows, cols, lambda a, b: (a, b ^ 2), crosses)

    def finish(turn):
        change = lambda a, b: target(turn)(a, b ^ 2)
        return moves(rows, cols, change, stays)

    move = lambda value, pairs: lax.ppermute(value, AXES, pairs)
    straight = lambda turn: moves(rows, cols, target(turn))
    local = moves(rows, cols, target(0), stays)
    core = lax.rem(c, 2)

    two = sent(0, 1, 2)
    hop_two = move(two, hop)
    one = sent(0, 3, 1, (two,))
    hop_one = move(one, hop)
    local_two = move(two, local)
    direct_a = move(sent(1, 0, 2, (one,)), straight(1))
    near = pack_near((one,))
    core_near = move(near, over_core)

    spot = jnp.arange(3 * cut, dtype=jnp.int32)
    whose = jnp.minimum(spot // quarter, 1)
    tile = jnp.minimum((2 * side + core) * quarter + spot - whose * quarter, len(upper) - 1)
    picks = jnp.stack([jnp.where(whose == core, 0, 1), tile], axis=-1)
    far_1, far_2, far_3 = pack(
        functools.partial(pick_kernel, (cut,) * 3), picks, [near, core_near], width, (cut,) * 3,
        (hop_two, hop_one),
    )
    far_1 = move(far_1, over_y)
    crossed_two = move(hop_two, finish(0))
    (far_2,) = gate((far_2,), (far_1, direct_a, local_two))
    far_2 = move(far_2, over_y)
    side_1 = move(far_1, over_x)
    local_one = move(one, local)
    direct_b = move(sent(1, 2, 2, (direct_a,)), straight(1))
    far_3, hop_one = gate((far_3, hop_one), (far_2, crossed_two, local_one))
    far_3 = move(far_3, over_y)
    side_2 = move(far_2, over_x)
    crossed_one = move(hop_one, finish(0))
    (far_3,) = gate((far_3,), (direct_b,))
    side_3 = move(far_3, over_x)
    direct_c = move(sent(0, 0, 1, (direct_b,)), straight(0))
    core_far = [move(value, over_core) for value in (far_1, far_2, far_3)]
    core_side = [move(value, over_core) for value in (side_1, side_2)]

    is_far = vector >= 2 * held
    other = (number // quarter) ^ (2 * side + core)
    spot = (vector - 2 * held) * quarter + lax.rem(number, quarter)
    bank = jnp.where(is_far, 2 + 6 * (other % 2) + 3 * (other // 2) + spot // cut, vector)
    place = jnp.where(is_far, lax.rem(spot, cut), number)
    bank, place = jnp.broadcast_arrays(bank, place)
    pieces = [
        ((direct_c,), slice(0, 1)),
        ((crossed_two, local_two), slice(1, 3)),
        ((crossed_one, local_one), slice(3, 4)),
        ((direct_a,), slice(4, 6)),
        ((direct_b,), slice(6, 8)),
    ]

    def part(which, banks, chosen_vectors, total, adds):
        return ladder_part(
            amplitudes, tile_mask, [pieces[n][0] for n in which], banks,
            tables(bank, place, [pieces[n][1] for n in which], chosen_vectors), total, adds,
        )

    banks = [near, core_near]
    total = part([3, 1], banks, slice(0, 2), None, False)
    banks += [far_1, far_2, far_3, side_1, side_2, side_1] + core_far + core_side + core_side[:1]
    total = part([3, 1], banks, slice(2, 3), total, True)
    total = part([4, 2], banks, slice(0, 3), total, False)
    (side_3,) = gate((side_3,), (direct_c, total))
    banks[7] = side_3
    banks[13] = move(side_3, over_core)
    total = part([3, 1, 4, 2], banks, slice(3, 4), total, True)
    return part([0], banks, slice(0, 4), total, False)


def solution(mesh):
    return jax.shard_map(
        functools.partial(shards, mesh.shape["orow"], mesh.shape["ocol"]),
        mesh=mesh,
        in_specs=(
            P("orow", "ocol", None, None),
            P("orow", "ocol", None, None),
            P(),
            P("ocol", None, None),
        ),
        out_specs=P("orow", "ocol", None, None),
        check_vma=False,
    )
```

```python
import functools

import jax
import jax.numpy as jnp
from jax import lax
from jax.experimental import pallas as pl
from jax.experimental.pallas import tpu as pltpu
from jax.sharding import PartitionSpec as P

AXES = ("orow", "ocol")
ANY = pl.BlockSpec(memory_space=pl.ANY)
VMEM = 56 * 2**20


def pack_kernel(sizes, width, place_ref, source_ref, *refs):
    held, sems = refs[-2:]
    packed = refs[-2 - len(sizes) : -2]
    loads, stores = [], []
    for part, size in enumerate(sizes):
        for inside in range(size):
            n = len(loads)
            row = pl.multiple_of(place_ref[3 * n + 1] * width, width)
            col = pl.multiple_of(place_ref[3 * n + 2] * width, width)
            loads.append(
                pltpu.make_async_copy(
                    source_ref.at[place_ref[3 * n], pl.ds(row, width), pl.ds(col, width)],
                    held.at[n],
                    sems.at[0, n],
                )
            )
            stores.append(pltpu.make_async_copy(held.at[n], packed[part].at[inside], sems.at[1, n]))
    for load in loads:
        load.start()
    for load, store in zip(loads, stores):
        load.wait()
        store.start()
    for store in stores:
        store.wait()


def pack(places, cholesky, width, sizes, after=()):
    count, dtype = sum(sizes), cholesky.dtype
    return pl.pallas_call(
        functools.partial(pack_kernel, sizes, width),
        out_shape=[jax.ShapeDtypeStruct((size, width, width), dtype) for size in sizes],
        grid_spec=pltpu.PrefetchScalarGridSpec(
            num_scalar_prefetch=1,
            grid=(1,),
            in_specs=[ANY] * (1 + len(after)),
            out_specs=[ANY] * len(sizes),
            scratch_shapes=[
                pltpu.VMEM((count, width, width), dtype),
                pltpu.SemaphoreType.DMA((2, count)),
            ],
        ),
        compiler_params=pltpu.CompilerParams(vmem_limit_bytes=VMEM),
        cost_estimate=pl.CostEstimate(
            flops=0, bytes_accessed=count * width * width // 16, transcendentals=0
        ),
        name="pack_tiles",
    )(places.reshape(-1), cholesky, *after)


def keep_tiles(source, mask_ref, base, tiles, width, store):
    for a in range(tiles):
        for b in range(tiles):
            rows, cols = slice(a * width, (a + 1) * width), slice(b * width, (b + 1) * width)
            block = source[rows, cols]
            store(rows, cols, block * mask_ref[base + a * tiles + b].astype(block.dtype))


def send_kernel(tiles, width, rows, col_pairs, first, *refs):
    start_ref, mask_ref, amps_ref = refs[:3]
    out_ref = refs[-1]
    pair = first + pl.program_id(0)
    base = ((pair // rows) * col_pairs + start_ref[0] + lax.rem(pair, rows)) * tiles * tiles

    def store(rows, cols, value):
        out_ref[0, rows, cols] = value

    keep_tiles(amps_ref.at[0, 0], mask_ref, base, tiles, width, store)


def sent_pairs(amplitudes, tile_mask, col, first, count, after=()):
    rows, col_pairs, depth, _ = amplitudes.shape
    tiles = tile_mask.shape[-1]

    def source(i, start, mask):
        return (first + i) // rows, start[0] + lax.rem(first + i, rows), 0, 0

    return pl.pallas_call(
        functools.partial(send_kernel, tiles, depth // tiles, rows, col_pairs, first),
        out_shape=jax.ShapeDtypeStruct((count, depth, depth), amplitudes.dtype),
        grid_spec=pltpu.PrefetchScalarGridSpec(
            num_scalar_prefetch=2,
            grid=(count,),
            in_specs=[pl.BlockSpec((1, 1, depth, depth), source)] + [ANY] * len(after),
            out_specs=pl.BlockSpec((1, depth, depth), lambda i, start, mask: (i, 0, 0)),
        ),
        compiler_params=pltpu.CompilerParams(vmem_limit_bytes=VMEM),
        cost_estimate=pl.CostEstimate(
            flops=0, bytes_accessed=count * depth * depth // 16, transcendentals=0
        ),
        name="sent_pairs",
    )(col.reshape(1).astype(jnp.int32), tile_mask.reshape(-1), amplitudes, *after)


def ladder_kernel(tiles, width, counts, number, choices, early, added, col_pairs, *refs):
    bank_ref, place_ref, flip_ref, own_ref, mask_ref = refs[:5]
    amps_ref = refs[5]
    pieces, at = [], 6
    for arrays, pairs in counts:
        pieces.append((refs[at : at + arrays], pairs))
        at += arrays
    banks = refs[at : at + number]
    total_ref = refs[at + number] if added else None
    out_ref, factor, weighted, partner, sems = refs[-5:]
    pair, steps = pl.program_id(0), pl.num_programs(0)
    slots = [(a, b) for a in range(tiles) for b in range(a, tiles)]
    vectors = len(choices)

    def corner(index):
        return pl.ds(pl.multiple_of(index * width, width), width)

    def tile_of(bank, place):
        if bank.shape[-1] == width:
            return bank.at[place]
        across = bank.shape[-1] // width
        return bank.at[0, corner(place // across), corner(lax.rem(place, across))]

    def ends(which, pair):
        a, b = slots[which]
        if a == b:
            return a, b
        flip = flip_ref[pair * len(slots) + which]
        return a + flip * (b - a), b + flip * (a - b)

    def fetch(pair, slot, chosen):
        for vector in chosen:
            for which in range(len(slots)):
                entry = (pair * vectors + vector) * len(slots) + which
                row, col = ends(which, pair)

                def begin(n):
                    pltpu.make_async_copy(
                        tile_of(banks[n], place_ref[entry]),
                        factor.at[slot, vector, corner(row), corner(col)],
                        sems.at[slot, vector, which],
                    ).start()

                if len(choices[vector]) == 1:
                    begin(choices[vector][0])
                else:
                    for n in choices[vector]:
                        pl.when(bank_ref[entry] == n)(functools.partial(begin, n))

    def fetch_all(pair, slot):
        if added:
            pl.when(pair >= added)(lambda: fetch(pair, slot, range(early)))
        fetch(pair, slot, range(early if added else 0, vectors))

    slot = lax.rem(pair, 2)

    @pl.when(pair == 0)
    def _():
        fetch_all(pair, slot)

    @pl.when(pair + 1 < steps)
    def _():
        fetch_all(pair + 1, 1 - slot)

    def store(rows, cols, value):
        weighted[rows, cols] = value

    base = (own_ref[3 * pair] * col_pairs + own_ref[3 * pair + 1]) * tiles * tiles
    keep_tiles(amps_ref.at[0, 0], mask_ref, base, tiles, width, store)
    first = 0
    for arrays, pairs in pieces:
        @pl.when((pair >= first) & (pair < first + pairs))
        def _():
            for m, array in enumerate(arrays):
                @pl.when((own_ref[3 * pair + 2] == m) | (len(arrays) == 1))
                def _():
                    partner[...] = array[0]
        first += pairs

    def arrive(chosen):
        for vector in chosen:
            for which in range(len(slots)):
                row, col = ends(which, pair)
                pltpu.make_async_copy(
                    tile_of(banks[0], 0),
                    factor.at[slot, vector, corner(row), corner(col)],
                    sems.at[slot, vector, which],
                ).wait()
                if slots[which][0] != slots[which][1]:
                    factor[slot, vector, corner(col), corner(row)] = factor[
                        slot, vector, corner(row), corner(col)
                    ].T

    def products(chosen):
        total = None
        for vector in chosen:
            whole = factor[slot, vector]
            inner = jnp.dot(whole, weighted[...], preferred_element_type=jnp.float32)
            inner += lax.dot_general(
                whole, partner[...], (((1,), (1,)), ((), ())), preferred_element_type=jnp.float32
            )
            term = jnp.dot(inner.astype(jnp.bfloat16), whole, preferred_element_type=jnp.float32)
            total = term if total is None else total + term
        return total

    if not added:
        arrive(range(vectors))
        out_ref[0, 0] = products(range(vectors))
        return

    @pl.when(pair >= added)
    def _():
        arrive(range(early))
        out_ref[0, 0] = products(range(early))

    @pl.when(pair < added)
    def _():
        out_ref[0, 0] = total_ref[0, 0]

    arrive(range(early, vectors))
    out_ref[0, 0] += products(range(early, vectors))


def ladder_part(amplitudes, tile_mask, pieces, banks, choices, tables, total, early, added):
    bank, place, flip, own = tables
    pairs, vectors, slots = bank.shape
    tiles = tile_mask.shape[-1]
    col_pairs, depth = amplitudes.shape[1:3]
    width = depth // tiles
    block = (1, 1, depth, depth)

    def own_map(pair, bank, place, flip, own, mask):
        return own[3 * pair], own[3 * pair + 1], 0, 0

    def total_map(pair, bank, place, flip, own, mask):
        return own_map(jnp.minimum(pair, added - 1), bank, place, flip, own, mask)

    def piece_map(first, count, m, start):
        def index(pair, bank, place, flip, own, mask):
            inside = jnp.clip(pair - first, 0, count - 1)
            return start + jnp.where(own[3 * (first + inside) + 2] == m, inside, 0), 0, 0

        return index

    in_specs, operands, counts, first = [pl.BlockSpec(block, own_map)], [amplitudes], [], 0
    for arrays, count in pieces:
        for m, (array, start) in enumerate(arrays):
            in_specs.append(pl.BlockSpec((1, depth, depth), piece_map(first, count, m, start)))
            operands.append(array)
        counts.append((len(arrays), count))
        first += count
    in_specs += [ANY] * len(banks)
    operands += banks
    aliases = {}
    if total is not None:
        aliases = {5 + len(operands): 0}
        operands.append(total)
        in_specs.append(pl.BlockSpec(block, total_map) if added else ANY)
    flops = 6 * pairs * vectors * depth**3
    moved = pairs * (depth * depth * 8 + vectors * slots * width * width * 2)
    return pl.pallas_call(
        functools.partial(
            ladder_kernel, tiles, width, tuple(counts), len(banks), choices, early, added, col_pairs
        ),
        out_shape=jax.ShapeDtypeStruct(amplitudes.shape, jnp.float32),
        grid_spec=pltpu.PrefetchScalarGridSpec(
            num_scalar_prefetch=5,
            grid=(pairs,),
            in_specs=in_specs,
            out_specs=pl.BlockSpec(block, own_map),
            scratch_shapes=[
                pltpu.VMEM((2, vectors, depth, depth), jnp.bfloat16),
                pltpu.VMEM((depth, depth), jnp.bfloat16),
                pltpu.VMEM((depth, depth), jnp.bfloat16),
                pltpu.SemaphoreType.DMA((2, vectors, slots)),
            ],
        ),
        input_output_aliases=aliases,
        compiler_params=pltpu.CompilerParams(
            dimension_semantics=("arbitrary",), vmem_limit_bytes=VMEM
        ),
        cost_estimate=pl.CostEstimate(flops=flops // 64, bytes_accessed=moved // 64, transcendentals=0),
        name="ladder_part",
    )(
        bank.reshape(-1), place.reshape(-1), flip.reshape(-1), own.reshape(-1),
        tile_mask.reshape(-1), *operands,
    )


def gate_kernel(*refs):
    pass


def gate(values, after):
    return pl.pallas_call(
        gate_kernel,
        out_shape=[jax.ShapeDtypeStruct(value.shape, value.dtype) for value in values],
        in_specs=[ANY] * (len(values) + len(after)),
        out_specs=[ANY] * len(values),
        input_output_aliases={n: n for n in range(len(values))},
        compiler_params=pltpu.CompilerParams(vmem_limit_bytes=VMEM),
        cost_estimate=pl.CostEstimate(flops=0, bytes_accessed=0, transcendentals=0),
        name="gate",
    )(*values, *after)


def moves(rows, cols, change, chosen=lambda r, c: True):
    pairs = []
    for r in range(rows):
        for c in range(cols):
            if chosen(r, c):
                to_row, to_col = change(r, c)
                pairs.append((r * cols + c, to_row * cols + to_col))
    return pairs


def shards(rows, cols, amplitudes, tile_mask, domain_tiles, cholesky):
    row_pairs, col_pairs, depth, _ = amplitudes.shape
    tiles = domain_tiles.shape[-1]
    width = depth // tiles
    held = cholesky.shape[0]
    across = cholesky.shape[1] // width
    vectors = held * cols
    ratio = col_pairs // row_pairs
    r, c = lax.axis_index("orow"), lax.axis_index("ocol")

    paths = rows == 8 and cols == 4 and row_pairs == 2 and held == 1

    upper = [(s, t) for s in range(across) for t in range(s, across)]
    places = jnp.asarray([[q, s, t] for q in range(held) for s, t in upper], jnp.int32)
    cut = len(upper) * 7 // 36

    pair = jnp.arange(row_pairs * col_pairs, dtype=jnp.int32)
    turn = pair // (row_pairs * row_pairs)
    own_row = lax.rem(pair, row_pairs)
    own_col = lax.rem(r + ratio - turn, ratio) * row_pairs + lax.rem(pair // row_pairs, row_pairs)
    chosen = domain_tiles[r * row_pairs + own_row, c * col_pairs + own_col]
    corners = [(a, b) for a in range(tiles) for b in range(a, tiles)]
    first = jnp.stack([chosen[:, a] for a, _ in corners], axis=-1)
    second = jnp.stack([chosen[:, b] for _, b in corners], axis=-1)
    flip = (first > second).astype(jnp.int32)
    low, high = jnp.minimum(first, second), jnp.maximum(first, second)
    low, high = low[:, None, :], high[:, None, :]
    number = low * across - low * (low - 1) // 2 + high - low
    vector = jnp.arange(vectors, dtype=jnp.int32)[None, :, None]
    keeps = (c == r // ratio).astype(jnp.int32)
    at_home = jnp.where(r // 4 != c // 2, 0, 1 + keeps)
    source = jnp.where((turn > 0) | (not paths), 0, jnp.where(pair == 0, keeps, at_home))
    own = jnp.stack([own_row, own_col, source], axis=-1)
    side = lax.rem(r, 2)

    def target(turn):
        return lambda a, b: (ratio * b + (a + turn) % ratio, a // ratio)

    def sent(turn, first, count, after=()):
        col = lax.rem(r + turn, ratio) * row_pairs
        return sent_pairs(amplitudes, tile_mask, col, first, count, after)

    def tables(bank, place, which, chosen_vectors):
        return (
            jnp.concatenate([bank[w, chosen_vectors] for w in which]),
            jnp.concatenate([place[w, chosen_vectors] for w in which]),
            jnp.concatenate([flip[w] for w in which]),
            jnp.concatenate([own[w] for w in which]),
        )

    square = row_pairs * row_pairs
    if not paths:
        (packed,) = pack(places, cholesky, width, (len(places),))
        banks = [lax.all_gather(packed, "ocol", axis=0, tiled=True)]
        place = vector * len(upper) + number
        bank = jnp.zeros_like(place)
        pieces = [
            ([(lax.ppermute(sent(turn, 0, square), AXES, moves(rows, cols, target(turn))), 0)], square)
            for turn in range(ratio)
        ]
        every = tables(bank, place, [slice(None)], slice(None))
        choices = ((0,),) * vectors
        return ladder_part(amplitudes, tile_mask, pieces, banks, choices, every, None, 0, 0)

    crosses = lambda a, b: (a // 4) != (b // 2)
    stays = lambda a, b: not crosses(a, b)
    over_y = moves(rows, cols, lambda a, b: (a, b ^ 2))
    over_x = moves(rows, cols, lambda a, b: (a ^ 1, b))
    over_core = moves(rows, cols, lambda a, b: (a, b ^ 1))
    hop = moves(rows, cols, lambda a, b: (a, b ^ 2), crosses)

    def finish(turn):
        change = lambda a, b: target(turn)(a, b ^ 2)
        return moves(rows, cols, change, stays)

    move = lambda value, pairs: lax.ppermute(value, AXES, pairs)
    straight = lambda turn: moves(rows, cols, target(turn), lambda a, b: target(turn)(a, b) != (a, b))
    stay = moves(rows, cols, target(0), lambda a, b: stays(a, b) and target(0)(a, b) != (a, b))
    spot = side * (2 * cut) + jnp.arange(2 * cut, dtype=jnp.int32)

    core_near = move(cholesky, over_core)
    other = sent(0, 1, 3)
    hop_all = move(other, hop)
    far_1, far_2, far_3 = pack(
        jnp.concatenate([places[spot], places[4 * cut :]]), cholesky, width,
        (cut, cut, len(upper) - 4 * cut), (other,),
    )
    far_1 = move(far_1, over_y)
    direct_1 = move(sent(1, 0, 2, (other,)), straight(1))
    local = move(other, stay)
    far_2, direct_2 = gate((far_2, sent(1, 2, 1, (other,))), (far_1, direct_1, core_near))
    far_2 = move(far_2, over_y)
    side_1 = move(far_1, over_x)
    direct_2 = move(direct_2, straight(1))
    hops = [hop_all[n : n + 1] for n in range(3)]
    crossed_1 = move(hops[0], finish(0))
    core_far_1 = move(far_1, over_core)
    far_3, direct_3, crossed_2 = gate(
        (far_3, sent(1, 3, 1, (other,)), hops[1]),
        (far_2, side_1, direct_2, crossed_1, core_far_1, local),
    )
    far_3 = move(far_3, over_y)
    side_2 = move(far_2, over_x)
    direct_3 = move(direct_3, straight(1))
    crossed_2 = move(crossed_2, finish(0))
    core_far_2 = move(far_2, over_core)
    core_side_1 = move(side_1, over_core)

    is_far = vector >= 2
    theirs = jnp.where(number // (2 * cut) == side, 0, 2)
    inner = lax.rem(number, 2 * cut)
    last = number >= 4 * cut
    bank = jnp.where(is_far, 5 * vector - 8 + jnp.where(last, 4, theirs + inner // cut), vector)
    place = jnp.where(
        is_far, jnp.where(last, number - 4 * cut, lax.rem(inner, cut)), low * across + high
    )
    bank, place = jnp.broadcast_arrays(bank, place)
    choices = ((0,), (1,), (2, 3, 4, 5, 6), (7, 8, 9, 10, 11))
    banks = [cholesky, core_near]

    def part(which, vectors, total, added):
        pieces = [inputs[n] for n in which]
        spans = [slice(start, start + count) for start, _, count in pieces]
        return ladder_part(
            amplitudes, tile_mask, [piece[1:] for piece in pieces], banks, choices[:vectors],
            tables(bank, place, spans, slice(0, vectors)), total, 2, added,
        )

    inputs = {
        "straight 1": (4, [(direct_1, 0)], 2),
        "straight 2": (6, [(direct_2, 0)], 1),
        "straight 3": (7, [(direct_3, 0)], 1),
        "hop 1": (1, [(crossed_1, 0), (local, 0), (other, 0)], 1),
        "hop 2": (2, [(crossed_2, 0), (local, 1), (other, 1)], 1),
    }
    total = part(["straight 1", "straight 2", "hop 1"], 2, None, 0)
    single = sent(0, 0, 1, (other,))
    far_3, direct_4, crossed_3 = gate(
        (far_3, single, hops[2]), (side_2, direct_3, crossed_2, core_far_2, core_side_1, total)
    )
    core_far_3 = move(far_3, over_core)
    core_side_2 = move(side_2, over_core)
    kept = direct_4
    direct_4 = move(kept, straight(0))
    crossed_3 = move(crossed_3, finish(0))
    inputs["straight 4"] = (0, [(direct_4, 0), (kept, 0)], 1)
    inputs["hop 3"] = (3, [(crossed_3, 0), (local, 2), (other, 2)], 1)
    banks += [far_1, far_2, side_1, side_2, far_3]
    banks += [core_far_1, core_far_2, core_side_1, core_side_2, core_far_3]
    total = part(["straight 1", "straight 2", "hop 1", "straight 3", "hop 2"], 4, total, 4)
    return part(["straight 4", "hop 3"], 4, total, 0)


def solution(mesh):
    return jax.shard_map(
        functools.partial(shards, mesh.shape["orow"], mesh.shape["ocol"]),
        mesh=mesh,
        in_specs=(
            P("orow", "ocol", None, None),
            P("orow", "ocol", None, None),
            P(),
            P("ocol", None, None),
        ),
        out_specs=P("orow", "ocol", None, None),
        check_vma=False,
    )
```

```python
import functools

import jax
import jax.numpy as jnp
from jax import lax
from jax.experimental import pallas as pl
from jax.experimental.pallas import tpu as pltpu
from jax.sharding import PartitionSpec as P

AXES = ("orow", "ocol")
ANY = pl.BlockSpec(memory_space=pl.ANY)
VMEM = 56 * 2**20
DEEP = 3


def pack_kernel(sizes, width, place_ref, source_ref, *refs):
    held, sems = refs[-2:]
    packed = refs[-2 - len(sizes) : -2]
    loads, stores = [], []
    for part, size in enumerate(sizes):
        for inside in range(size):
            n = len(loads)
            row = pl.multiple_of(place_ref[3 * n + 1] * width, width)
            col = pl.multiple_of(place_ref[3 * n + 2] * width, width)
            loads.append(
                pltpu.make_async_copy(
                    source_ref.at[place_ref[3 * n], pl.ds(row, width), pl.ds(col, width)],
                    held.at[n],
                    sems.at[0, n],
                )
            )
            stores.append(pltpu.make_async_copy(held.at[n], packed[part].at[inside], sems.at[1, n]))
    for load in loads:
        load.start()
    for load, store in zip(loads, stores):
        load.wait()
        store.start()
    for store in stores:
        store.wait()


def pack(places, cholesky, width, sizes, after=()):
    count, dtype = sum(sizes), cholesky.dtype
    return pl.pallas_call(
        functools.partial(pack_kernel, sizes, width),
        out_shape=[jax.ShapeDtypeStruct((size, width, width), dtype) for size in sizes],
        grid_spec=pltpu.PrefetchScalarGridSpec(
            num_scalar_prefetch=1,
            grid=(1,),
            in_specs=[ANY] * (1 + len(after)),
            out_specs=[ANY] * len(sizes),
            scratch_shapes=[
                pltpu.VMEM((count, width, width), dtype),
                pltpu.SemaphoreType.DMA((2, count)),
            ],
        ),
        compiler_params=pltpu.CompilerParams(vmem_limit_bytes=VMEM),
        cost_estimate=pl.CostEstimate(
            flops=0, bytes_accessed=count * width * width // 16, transcendentals=0
        ),
        name="pack_tiles",
    )(places.reshape(-1), cholesky, *after)


def keep_tiles(source, mask_ref, base, tiles, width, store):
    for a in range(tiles):
        for b in range(tiles):
            rows, cols = slice(a * width, (a + 1) * width), slice(b * width, (b + 1) * width)
            block = source[rows, cols]
            store(rows, cols, block * mask_ref[base + a * tiles + b].astype(block.dtype))


def send_kernel(tiles, width, rows, col_pairs, first, *refs):
    start_ref, mask_ref, amps_ref = refs[:3]
    out_ref = refs[-1]
    pair = first + pl.program_id(0)
    base = ((pair // rows) * col_pairs + start_ref[0] + lax.rem(pair, rows)) * tiles * tiles

    def store(rows, cols, value):
        out_ref[0, rows, cols] = value

    keep_tiles(amps_ref.at[0, 0], mask_ref, base, tiles, width, store)


def sent_pairs(amplitudes, tile_mask, col, first, count, after=()):
    rows, col_pairs, depth, _ = amplitudes.shape
    tiles = tile_mask.shape[-1]

    def source(i, start, mask):
        return (first + i) // rows, start[0] + lax.rem(first + i, rows), 0, 0

    return pl.pallas_call(
        functools.partial(send_kernel, tiles, depth // tiles, rows, col_pairs, first),
        out_shape=jax.ShapeDtypeStruct((count, depth, depth), amplitudes.dtype),
        grid_spec=pltpu.PrefetchScalarGridSpec(
            num_scalar_prefetch=2,
            grid=(count,),
            in_specs=[pl.BlockSpec((1, 1, depth, depth), source)] + [ANY] * len(after),
            out_specs=pl.BlockSpec((1, depth, depth), lambda i, start, mask: (i, 0, 0)),
        ),
        compiler_params=pltpu.CompilerParams(vmem_limit_bytes=VMEM),
        cost_estimate=pl.CostEstimate(
            flops=0, bytes_accessed=count * depth * depth // 16, transcendentals=0
        ),
        name="sent_pairs",
    )(col.reshape(1).astype(jnp.int32), tile_mask.reshape(-1), amplitudes, *after)


def ladder_kernel(tiles, width, counts, number, choices, early, added, col_pairs, *refs):
    bank_ref, place_ref, flip_ref, own_ref, mask_ref = refs[:5]
    amps_ref = refs[5]
    pieces, at = [], 6
    for starts, pairs in counts:
        pieces.append((refs[at : at + len(starts)], starts, pairs))
        at += len(starts)
    banks = refs[at : at + number]
    total_ref = refs[at + number] if added else None
    out_ref, factor, weighted, partner, sems, partner_sems = refs[-6:]
    pair, steps = pl.program_id(0), pl.num_programs(0)
    slots = [(a, b) for a in range(tiles) for b in range(a, tiles)]
    vectors = len(choices)

    def corner(index):
        return pl.ds(pl.multiple_of(index * width, width), width)

    def tile_of(bank, place):
        if bank.shape[-1] == width:
            return bank.at[place]
        across = bank.shape[-1] // width
        return bank.at[0, corner(place // across), corner(lax.rem(place, across))]

    def ends(which, pair):
        a, b = slots[which]
        if a == b:
            return a, b
        flip = flip_ref[pair * len(slots) + which]
        return a + flip * (b - a), b + flip * (a - b)

    def fetch(pair, slot, chosen):
        for vector in chosen:
            for which in range(len(slots)):
                entry = (pair * vectors + vector) * len(slots) + which
                row, col = ends(which, pair)

                def begin(n):
                    pltpu.make_async_copy(
                        tile_of(banks[n], place_ref[entry]),
                        factor.at[slot, vector, corner(row), corner(col)],
                        sems.at[slot, vector, which],
                    ).start()

                if len(choices[vector]) == 1:
                    begin(choices[vector][0])
                else:
                    for n in choices[vector]:
                        pl.when(bank_ref[entry] == n)(functools.partial(begin, n))

    def fetch_partner(pair, slot):
        first = 0
        for arrays, starts, pairs in pieces:
            for m, (array, start) in enumerate(zip(arrays, starts)):
                here = (pair >= first) & (pair < first + pairs)
                if len(arrays) > 1:
                    here &= own_ref[3 * pair + 2] == m

                @pl.when(here)
                def _():
                    pltpu.make_async_copy(
                        array.at[start + pair - first], partner.at[slot], partner_sems.at[slot]
                    ).start()
            first += pairs

    def fetch_all(pair, slot):
        fetch_partner(pair, slot)
        if added:
            pl.when(pair >= added)(lambda: fetch(pair, slot, range(early)))
        fetch(pair, slot, range(early if added else 0, vectors))

    slot = lax.rem(pair, DEEP)

    @pl.when(pair == 0)
    def _():
        for n in range(DEEP - 1):
            pl.when(n < steps)(functools.partial(fetch_all, pair + n, n))

    @pl.when(pair + DEEP - 1 < steps)
    def _():
        fetch_all(pair + DEEP - 1, lax.rem(pair + DEEP - 1, DEEP))

    def store(rows, cols, value):
        weighted[rows, cols] = value

    base = (own_ref[3 * pair] * col_pairs + own_ref[3 * pair + 1]) * tiles * tiles
    keep_tiles(amps_ref.at[0, 0], mask_ref, base, tiles, width, store)
    pltpu.make_async_copy(
        pieces[0][0][0].at[0], partner.at[slot], partner_sems.at[slot]
    ).wait()

    def arrive(chosen):
        for vector in chosen:
            for which in range(len(slots)):
                row, col = ends(which, pair)
                pltpu.make_async_copy(
                    tile_of(banks[0], 0),
                    factor.at[slot, vector, corner(row), corner(col)],
                    sems.at[slot, vector, which],
                ).wait()
                if slots[which][0] != slots[which][1]:
                    factor[slot, vector, corner(col), corner(row)] = factor[
                        slot, vector, corner(row), corner(col)
                    ].T

    def products(chosen):
        total = None
        for vector in chosen:
            whole = factor[slot, vector]
            inner = jnp.dot(whole, weighted[...], preferred_element_type=jnp.float32)
            inner += lax.dot_general(
                whole, partner[slot], (((1,), (1,)), ((), ())), preferred_element_type=jnp.float32
            )
            term = jnp.dot(inner.astype(jnp.bfloat16), whole, preferred_element_type=jnp.float32)
            total = term if total is None else total + term
        return total

    if not added:
        arrive(range(vectors))
        out_ref[0, 0] = products(range(vectors))
        return

    @pl.when(pair < added)
    def _():
        arrive(range(early, vectors))
        out_ref[0, 0] = total_ref[0, 0] + products(range(early, vectors))

    @pl.when(pair >= added)
    def _():
        arrive(range(vectors))
        out_ref[0, 0] = products(range(vectors))


def ladder_part(amplitudes, tile_mask, pieces, banks, choices, tables, total, early, added):
    bank, place, flip, own = tables
    pairs, vectors, slots = bank.shape
    tiles = tile_mask.shape[-1]
    col_pairs, depth = amplitudes.shape[1:3]
    width = depth // tiles
    block = (1, 1, depth, depth)

    def own_map(pair, bank, place, flip, own, mask):
        return own[3 * pair], own[3 * pair + 1], 0, 0

    def total_map(pair, bank, place, flip, own, mask):
        return own_map(jnp.minimum(pair, added - 1), bank, place, flip, own, mask)

    in_specs, operands, counts = [pl.BlockSpec(block, own_map)], [amplitudes], []
    for arrays, count in pieces:
        for array, _ in arrays:
            in_specs.append(ANY)
            operands.append(array)
        counts.append((tuple(start for _, start in arrays), count))
    in_specs += [ANY] * len(banks)
    operands += banks
    aliases = {}
    if total is not None:
        aliases = {5 + len(operands): 0}
        operands.append(total)
        in_specs.append(pl.BlockSpec(block, total_map) if added else ANY)
    flops = 6 * pairs * vectors * depth**3
    moved = pairs * (depth * depth * 8 + vectors * slots * width * width * 2)
    return pl.pallas_call(
        functools.partial(
            ladder_kernel, tiles, width, tuple(counts), len(banks), choices, early, added, col_pairs
        ),
        out_shape=jax.ShapeDtypeStruct(amplitudes.shape, jnp.float32),
        grid_spec=pltpu.PrefetchScalarGridSpec(
            num_scalar_prefetch=5,
            grid=(pairs,),
            in_specs=in_specs,
            out_specs=pl.BlockSpec(block, own_map),
            scratch_shapes=[
                pltpu.VMEM((DEEP, vectors, depth, depth), jnp.bfloat16),
                pltpu.VMEM((depth, depth), jnp.bfloat16),
                pltpu.VMEM((DEEP, depth, depth), jnp.bfloat16),
                pltpu.SemaphoreType.DMA((DEEP, vectors, slots)),
                pltpu.SemaphoreType.DMA((DEEP,)),
            ],
        ),
        input_output_aliases=aliases,
        compiler_params=pltpu.CompilerParams(
            dimension_semantics=("arbitrary",), vmem_limit_bytes=VMEM
        ),
        cost_estimate=pl.CostEstimate(flops=flops // 64, bytes_accessed=moved // 64, transcendentals=0),
        name="ladder_part",
    )(
        bank.reshape(-1), place.reshape(-1), flip.reshape(-1), own.reshape(-1),
        tile_mask.reshape(-1), *operands,
    )


def gate_kernel(*refs):
    pass


def gate(values, after):
    return pl.pallas_call(
        gate_kernel,
        out_shape=[jax.ShapeDtypeStruct(value.shape, value.dtype) for value in values],
        in_specs=[ANY] * (len(values) + len(after)),
        out_specs=[ANY] * len(values),
        input_output_aliases={n: n for n in range(len(values))},
        compiler_params=pltpu.CompilerParams(vmem_limit_bytes=VMEM),
        cost_estimate=pl.CostEstimate(flops=0, bytes_accessed=0, transcendentals=0),
        name="gate",
    )(*values, *after)


def moves(rows, cols, change, chosen=lambda r, c: True):
    pairs = []
    for r in range(rows):
        for c in range(cols):
            if chosen(r, c):
                to_row, to_col = change(r, c)
                pairs.append((r * cols + c, to_row * cols + to_col))
    return pairs


def shards(rows, cols, amplitudes, tile_mask, domain_tiles, cholesky):
    row_pairs, col_pairs, depth, _ = amplitudes.shape
    tiles = domain_tiles.shape[-1]
    width = depth // tiles
    held = cholesky.shape[0]
    across = cholesky.shape[1] // width
    vectors = held * cols
    ratio = col_pairs // row_pairs
    r, c = lax.axis_index("orow"), lax.axis_index("ocol")

    paths = rows == 8 and cols == 4 and row_pairs == 2 and held == 1

    upper = [(s, t) for s in range(across) for t in range(s, across)]
    places = jnp.asarray([[q, s, t] for q in range(held) for s, t in upper], jnp.int32)
    first_cut, second_cut = len(upper) * 7 // 36, len(upper) * 8 // 36
    both = first_cut + second_cut

    pair = jnp.arange(row_pairs * col_pairs, dtype=jnp.int32)
    turn = pair // (row_pairs * row_pairs)
    own_row = lax.rem(pair, row_pairs)
    own_col = lax.rem(r + ratio - turn, ratio) * row_pairs + lax.rem(pair // row_pairs, row_pairs)
    chosen = domain_tiles[r * row_pairs + own_row, c * col_pairs + own_col]
    corners = [(a, b) for a in range(tiles) for b in range(a, tiles)]
    first = jnp.stack([chosen[:, a] for a, _ in corners], axis=-1)
    second = jnp.stack([chosen[:, b] for _, b in corners], axis=-1)
    flip = (first > second).astype(jnp.int32)
    low, high = jnp.minimum(first, second), jnp.maximum(first, second)
    low, high = low[:, None, :], high[:, None, :]
    number = low * across - low * (low - 1) // 2 + high - low
    vector = jnp.arange(vectors, dtype=jnp.int32)[None, :, None]
    keeps = (c == r // ratio).astype(jnp.int32)
    at_home = (r // 4 == c // 2).astype(jnp.int32)
    source = jnp.where(turn == 0, keeps, jnp.where(pair == row_pairs**2, 0, at_home))
    source = jnp.where(paths, source, 0)
    own = jnp.stack([own_row, own_col, source], axis=-1)
    side = lax.rem(r, 2)

    def target(turn):
        return lambda a, b: (ratio * b + (a + turn) % ratio, a // ratio)

    def sent(turn, first, count, after=()):
        col = lax.rem(r + turn, ratio) * row_pairs
        return sent_pairs(amplitudes, tile_mask, col, first, count, after)

    def tables(bank, place, which, chosen_vectors):
        return (
            jnp.concatenate([bank[w, chosen_vectors] for w in which]),
            jnp.concatenate([place[w, chosen_vectors] for w in which]),
            jnp.concatenate([flip[w] for w in which]),
            jnp.concatenate([own[w] for w in which]),
        )

    square = row_pairs * row_pairs
    if not paths:
        (packed,) = pack(places, cholesky, width, (len(places),))
        banks = [lax.all_gather(packed, "ocol", axis=0, tiled=True)]
        place = vector * len(upper) + number
        bank = jnp.zeros_like(place)
        pieces = [
            ([(lax.ppermute(sent(turn, 0, square), AXES, moves(rows, cols, target(turn))), 0)], square)
            for turn in range(ratio)
        ]
        every = tables(bank, place, [slice(None)], slice(None))
        choices = ((0,),) * vectors
        return ladder_part(amplitudes, tile_mask, pieces, banks, choices, every, None, 0, 0)

    crosses = lambda a, b: (a // 4) != (b // 2)
    stays = lambda a, b: not crosses(a, b)
    over_y = moves(rows, cols, lambda a, b: (a, b ^ 2))
    over_x = moves(rows, cols, lambda a, b: (a ^ 1, b))
    over_core = moves(rows, cols, lambda a, b: (a, b ^ 1))
    hop = moves(rows, cols, lambda a, b: (a ^ 1, b ^ 2), crosses)

    finish = moves(rows, cols, lambda a, b: target(1)(a ^ 1, b ^ 2), stays)

    move = lambda value, pairs: lax.ppermute(value, AXES, pairs)
    straight = lambda turn: moves(rows, cols, target(turn), lambda a, b: target(turn)(a, b) != (a, b))
    stay = moves(rows, cols, target(1), stays)
    spot = side * both + jnp.arange(both, dtype=jnp.int32)

    core_near = move(cholesky, over_core)
    other = sent(1, 1, 3)
    hop_all = move(other, hop)
    far_1, far_2, far_3 = pack(
        jnp.concatenate([places[spot], places[2 * both :]]), cholesky, width,
        (first_cut, second_cut, len(upper) - 2 * both), (other,),
    )
    far_1 = move(far_1, over_y)
    kept_1 = sent(0, 0, 2, (other,))
    direct_1 = move(kept_1, straight(0))
    local = move(other, stay)
    kept_2, kept_3, direct_4 = sent(0, 2, 1, (other,)), sent(0, 3, 1, (other,)), sent(1, 0, 1, (other,))
    far_1, far_2, kept_2, kept_3, direct_4 = gate(
        (far_1, far_2, kept_2, kept_3, direct_4), (direct_1, core_near, local)
    )
    far_2 = move(far_2, over_y)
    side_1 = move(far_1, over_x)
    direct_2 = move(kept_2, straight(0))
    hops = [hop_all[n : n + 1] for n in range(3)]
    crossed_1 = move(hops[0], finish)
    core_far_1 = move(far_1, over_core)
    far_2, far_3, kept_3, crossed_2 = gate(
        (far_2, far_3, kept_3, hops[1]),
        (side_1, direct_2, crossed_1, core_far_1),
    )
    far_3 = move(far_3, over_y)
    side_2 = move(far_2, over_x)
    direct_3 = move(kept_3, straight(0))
    crossed_2 = move(crossed_2, finish)
    core_far_2 = move(far_2, over_core)

    is_far = vector >= 2
    theirs = jnp.where(number // both == side, 0, 2)
    inner = lax.rem(number, both)
    second = (inner >= first_cut).astype(jnp.int32)
    last = number >= 2 * both
    bank = jnp.where(is_far, 5 * vector - 8 + jnp.where(last, 4, theirs + second), vector)
    place = jnp.where(
        is_far, jnp.where(last, number - 2 * both, inner - second * first_cut), low * across + high
    )
    bank, place = jnp.broadcast_arrays(bank, place)
    choices = ((0,), (1,), (2, 3, 4, 5, 6), (7, 8, 9, 10, 11))
    banks = [cholesky, core_near]

    def part(which, vectors, total, added):
        pieces = [inputs[n] for n in which]
        spans = [slice(start, start + count) for start, _, count in pieces]
        return ladder_part(
            amplitudes, tile_mask, [piece[1:] for piece in pieces], banks, choices[:vectors],
            tables(bank, place, spans, slice(0, vectors)), total, 2, added,
        )

    inputs = {
        "straight 1": (0, [(direct_1, 0), (kept_1, 0)], 2),
        "straight 2": (2, [(direct_2, 0), (kept_2, 0)], 1),
        "straight 3": (3, [(direct_3, 0), (kept_3, 0)], 1),
        "hop 1": (5, [(crossed_1, 0), (local, 0)], 1),
        "hop 2": (6, [(crossed_2, 0), (local, 1)], 1),
    }
    total = part(["straight 1", "straight 2", "hop 1"], 2, None, 0)
    side_1, side_2, far_3, direct_4, crossed_3 = gate(
        (side_1, side_2, far_3, direct_4, hops[2]),
        (direct_3, crossed_2, core_far_2, total),
    )
    core_far_3 = move(far_3, over_core)
    core_side_1, core_side_2 = move(side_1, over_core), move(side_2, over_core)
    direct_4 = move(direct_4, straight(1))
    crossed_3 = move(crossed_3, finish)
    inputs["straight 4"] = (4, [(direct_4, 0)], 1)
    inputs["hop 3"] = (7, [(crossed_3, 0), (local, 2)], 1)
    banks += [far_1, far_2, side_1, side_2, far_3]
    banks += [core_far_1, core_far_2, core_side_1, core_side_2, core_far_3]
    total = part(["straight 1", "straight 2", "hop 1", "straight 3", "hop 2"], 4, total, 4)
    return part(["straight 4", "hop 3"], 4, total, 0)


def solution(mesh):
    return jax.shard_map(
        functools.partial(shards, mesh.shape["orow"], mesh.shape["ocol"]),
        mesh=mesh,
        in_specs=(
            P("orow", "ocol", None, None),
            P("orow", "ocol", None, None),
            P(),
            P("ocol", None, None),
        ),
        out_specs=P("orow", "ocol", None, None),
        check_vma=False,
    )
```

```python
import functools

import jax
import jax.numpy as jnp
from jax import lax
from jax.experimental import pallas as pl
from jax.experimental.pallas import tpu as pltpu
from jax.sharding import PartitionSpec as P

AXES = ("orow", "ocol")
ANY = pl.BlockSpec(memory_space=pl.ANY)
VMEM = 56 * 2**20
DEEP = 3


def pack_kernel(sizes, width, place_ref, source_ref, *refs):
    held, sems = refs[-2:]
    packed = refs[-2 - len(sizes) : -2]
    loads, stores = [], []
    for part, size in enumerate(sizes):
        for inside in range(size):
            n = len(loads)
            row = pl.multiple_of(place_ref[3 * n + 1] * width, width)
            col = pl.multiple_of(place_ref[3 * n + 2] * width, width)
            loads.append(
                pltpu.make_async_copy(
                    source_ref.at[place_ref[3 * n], pl.ds(row, width), pl.ds(col, width)],
                    held.at[n],
                    sems.at[0, n],
                )
            )
            stores.append(pltpu.make_async_copy(held.at[n], packed[part].at[inside], sems.at[1, n]))
    for load in loads:
        load.start()
    for load, store in zip(loads, stores):
        load.wait()
        store.start()
    for store in stores:
        store.wait()


def pack(places, cholesky, width, sizes, after=()):
    count, dtype = sum(sizes), cholesky.dtype
    return pl.pallas_call(
        functools.partial(pack_kernel, sizes, width),
        out_shape=[jax.ShapeDtypeStruct((size, width, width), dtype) for size in sizes],
        grid_spec=pltpu.PrefetchScalarGridSpec(
            num_scalar_prefetch=1,
            grid=(1,),
            in_specs=[ANY] * (1 + len(after)),
            out_specs=[ANY] * len(sizes),
            scratch_shapes=[
                pltpu.VMEM((count, width, width), dtype),
                pltpu.SemaphoreType.DMA((2, count)),
            ],
        ),
        compiler_params=pltpu.CompilerParams(vmem_limit_bytes=VMEM),
        cost_estimate=pl.CostEstimate(
            flops=0, bytes_accessed=count * width * width // 16, transcendentals=0
        ),
        name="pack_tiles",
    )(places.reshape(-1), cholesky, *after)


def keep_tiles(source, mask_ref, base, tiles, width, store):
    for a in range(tiles):
        for b in range(tiles):
            rows, cols = slice(a * width, (a + 1) * width), slice(b * width, (b + 1) * width)
            block = source[rows, cols]
            store(rows, cols, block * mask_ref[base + a * tiles + b].astype(block.dtype))


def send_kernel(tiles, width, rows, col_pairs, first, *refs):
    start_ref, mask_ref, amps_ref = refs[:3]
    out_ref = refs[-1]
    pair = first + pl.program_id(0)
    base = ((pair // rows) * col_pairs + start_ref[0] + lax.rem(pair, rows)) * tiles * tiles

    def store(rows, cols, value):
        out_ref[0, rows, cols] = value

    keep_tiles(amps_ref.at[0, 0], mask_ref, base, tiles, width, store)


def sent_pairs(amplitudes, tile_mask, col, first, count, after=()):
    rows, col_pairs, depth, _ = amplitudes.shape
    tiles = tile_mask.shape[-1]

    def source(i, start, mask):
        return (first + i) // rows, start[0] + lax.rem(first + i, rows), 0, 0

    return pl.pallas_call(
        functools.partial(send_kernel, tiles, depth // tiles, rows, col_pairs, first),
        out_shape=jax.ShapeDtypeStruct((count, depth, depth), amplitudes.dtype),
        grid_spec=pltpu.PrefetchScalarGridSpec(
            num_scalar_prefetch=2,
            grid=(count,),
            in_specs=[pl.BlockSpec((1, 1, depth, depth), source)] + [ANY] * len(after),
            out_specs=pl.BlockSpec((1, depth, depth), lambda i, start, mask: (i, 0, 0)),
        ),
        compiler_params=pltpu.CompilerParams(vmem_limit_bytes=VMEM),
        cost_estimate=pl.CostEstimate(
            flops=0, bytes_accessed=count * depth * depth // 16, transcendentals=0
        ),
        name="sent_pairs",
    )(col.reshape(1).astype(jnp.int32), tile_mask.reshape(-1), amplitudes, *after)


class View:
    def __init__(self, ref, start):
        self.ref, self.start = ref, start

    def __getitem__(self, index):
        return self.ref[self.start + index]


def ladder_kernel(tiles, width, counts, number, choices, early, added, col_pairs, starts, *refs):
    table_ref, amps_ref = refs[:2]
    base_pair, stride = starts[:2]
    slots = [(a, b) for a in range(tiles) for b in range(a, tiles)]
    bank_ref, place_ref = (View(table_ref, start + base_pair * stride * len(slots)) for start in starts[2:4])
    flip_ref = View(table_ref, starts[4] + base_pair * len(slots))
    own_ref, mask_ref = View(table_ref, starts[5] + 3 * base_pair), View(table_ref, starts[6])
    pieces, at = [], 2
    for firsts, pairs in counts:
        pieces.append((refs[at : at + len(firsts)], firsts, pairs))
        at += len(firsts)
    banks = refs[at : at + number]
    total_ref = refs[at + number] if added else None
    out_ref, factor, weighted, partner, sems, partner_sems = refs[-6:]
    pair, steps = pl.program_id(0), pl.num_programs(0)
    vectors = len(choices)

    def corner(index):
        return pl.ds(pl.multiple_of(index * width, width), width)

    def tile_of(bank, place):
        if bank.shape[-1] == width:
            return bank.at[place]
        across = bank.shape[-1] // width
        return bank.at[0, corner(place // across), corner(lax.rem(place, across))]

    def ends(which, pair):
        a, b = slots[which]
        if a == b:
            return a, b
        flip = flip_ref[pair * len(slots) + which]
        return a + flip * (b - a), b + flip * (a - b)

    def fetch(pair, slot, chosen):
        for vector in chosen:
            for which in range(len(slots)):
                entry = (pair * stride + vector) * len(slots) + which
                row, col = ends(which, pair)

                def begin(n):
                    pltpu.make_async_copy(
                        tile_of(banks[n], place_ref[entry]),
                        factor.at[slot, vector, corner(row), corner(col)],
                        sems.at[slot, vector, which],
                    ).start()

                if len(choices[vector]) == 1:
                    begin(choices[vector][0])
                else:
                    for n in choices[vector]:
                        pl.when(bank_ref[entry] == n)(functools.partial(begin, n))

    def fetch_partner(pair, slot):
        first = 0
        for arrays, firsts, pairs in pieces:
            for m, (array, start) in enumerate(zip(arrays, firsts)):
                here = (pair >= first) & (pair < first + pairs)
                if len(arrays) > 1:
                    here &= own_ref[3 * pair + 2] == m

                @pl.when(here)
                def _():
                    pltpu.make_async_copy(
                        array.at[start + pair - first], partner.at[slot], partner_sems.at[slot]
                    ).start()
            first += pairs

    def fetch_all(pair, slot):
        fetch_partner(pair, slot)
        if added:
            pl.when(pair >= added)(lambda: fetch(pair, slot, range(early)))
        fetch(pair, slot, range(early if added else 0, vectors))

    slot = lax.rem(pair, DEEP)

    @pl.when(pair == 0)
    def _():
        for n in range(DEEP - 1):
            pl.when(n < steps)(functools.partial(fetch_all, pair + n, n))

    @pl.when(pair + DEEP - 1 < steps)
    def _():
        fetch_all(pair + DEEP - 1, lax.rem(pair + DEEP - 1, DEEP))

    def store(rows, cols, value):
        weighted[rows, cols] = value

    base = (own_ref[3 * pair] * col_pairs + own_ref[3 * pair + 1]) * tiles * tiles
    keep_tiles(amps_ref.at[0, 0], mask_ref, base, tiles, width, store)
    pltpu.make_async_copy(
        pieces[0][0][0].at[0], partner.at[slot], partner_sems.at[slot]
    ).wait()

    def arrive(chosen):
        for vector in chosen:
            for which in range(len(slots)):
                row, col = ends(which, pair)
                pltpu.make_async_copy(
                    tile_of(banks[0], 0),
                    factor.at[slot, vector, corner(row), corner(col)],
                    sems.at[slot, vector, which],
                ).wait()
                if slots[which][0] != slots[which][1]:
                    factor[slot, vector, corner(col), corner(row)] = factor[
                        slot, vector, corner(row), corner(col)
                    ].T

    def products(chosen):
        total = None
        for vector in chosen:
            whole = factor[slot, vector]
            inner = jnp.dot(whole, weighted[...], preferred_element_type=jnp.float32)
            inner += lax.dot_general(
                whole, partner[slot], (((1,), (1,)), ((), ())), preferred_element_type=jnp.float32
            )
            term = jnp.dot(inner.astype(jnp.bfloat16), whole, preferred_element_type=jnp.float32)
            total = term if total is None else total + term
        return total

    if not added:
        arrive(range(vectors))
        out_ref[0, 0] = products(range(vectors))
        return

    @pl.when(pair < added)
    def _():
        arrive(range(early, vectors))
        out_ref[0, 0] = total_ref[0, 0] + products(range(early, vectors))

    @pl.when(pair >= added)
    def _():
        arrive(range(vectors))
        out_ref[0, 0] = products(range(vectors))


def ladder_part(amplitudes, tiles, pieces, banks, choices, table, starts, total, early, added):
    pairs, vectors = sum(count for _, count in pieces), len(choices)
    slots = tiles * (tiles + 1) // 2
    col_pairs, depth = amplitudes.shape[1:3]
    width = depth // tiles
    block = (1, 1, depth, depth)

    def own_map(pair, table):
        own = starts[5] + 3 * (starts[0] + pair)
        return table[own], table[own + 1], 0, 0

    def total_map(pair, table):
        return own_map(jnp.minimum(pair, added - 1), table)

    in_specs, operands, counts = [pl.BlockSpec(block, own_map)], [amplitudes], []
    for arrays, count in pieces:
        for array, _ in arrays:
            in_specs.append(ANY)
            operands.append(array)
        counts.append((tuple(start for _, start in arrays), count))
    in_specs += [ANY] * len(banks)
    operands += banks
    aliases = {}
    if total is not None:
        aliases = {1 + len(operands): 0}
        operands.append(total)
        in_specs.append(pl.BlockSpec(block, total_map) if added else ANY)
    flops = 6 * pairs * vectors * depth**3
    moved = pairs * (depth * depth * 8 + vectors * slots * width * width * 2)
    return pl.pallas_call(
        functools.partial(
            ladder_kernel, tiles, width, tuple(counts), len(banks), choices, early, added, col_pairs,
            starts,
        ),
        out_shape=jax.ShapeDtypeStruct(amplitudes.shape, jnp.float32),
        grid_spec=pltpu.PrefetchScalarGridSpec(
            num_scalar_prefetch=1,
            grid=(pairs,),
            in_specs=in_specs,
            out_specs=pl.BlockSpec(block, own_map),
            scratch_shapes=[
                pltpu.VMEM((DEEP, vectors, depth, depth), jnp.bfloat16),
                pltpu.VMEM((depth, depth), jnp.bfloat16),
                pltpu.VMEM((DEEP, depth, depth), jnp.bfloat16),
                pltpu.SemaphoreType.DMA((DEEP, vectors, slots)),
                pltpu.SemaphoreType.DMA((DEEP,)),
            ],
        ),
        input_output_aliases=aliases,
        compiler_params=pltpu.CompilerParams(
            dimension_semantics=("arbitrary",), vmem_limit_bytes=VMEM
        ),
        cost_estimate=pl.CostEstimate(flops=flops // 64, bytes_accessed=moved // 64, transcendentals=0),
        name="ladder_part",
    )(table, *operands)


def gate_kernel(*refs):
    pass


def gate(values, after):
    return pl.pallas_call(
        gate_kernel,
        out_shape=[jax.ShapeDtypeStruct(value.shape, value.dtype) for value in values],
        in_specs=[ANY] * (len(values) + len(after)),
        out_specs=[ANY] * len(values),
        input_output_aliases={n: n for n in range(len(values))},
        compiler_params=pltpu.CompilerParams(vmem_limit_bytes=VMEM),
        cost_estimate=pl.CostEstimate(flops=0, bytes_accessed=0, transcendentals=0),
        name="gate",
    )(*values, *after)


def moves(rows, cols, change, chosen=lambda r, c: True):
    pairs = []
    for r in range(rows):
        for c in range(cols):
            if chosen(r, c):
                to_row, to_col = change(r, c)
                pairs.append((r * cols + c, to_row * cols + to_col))
    return pairs


def shards(rows, cols, amplitudes, tile_mask, domain_tiles, cholesky):
    row_pairs, col_pairs, depth, _ = amplitudes.shape
    tiles = domain_tiles.shape[-1]
    width = depth // tiles
    held = cholesky.shape[0]
    across = cholesky.shape[1] // width
    vectors = held * cols
    ratio = col_pairs // row_pairs
    r, c = lax.axis_index("orow"), lax.axis_index("ocol")

    paths = rows == 8 and cols == 4 and row_pairs == 2 and held == 1

    upper = [(s, t) for s in range(across) for t in range(s, across)]
    places = jnp.asarray([[q, s, t] for q in range(held) for s, t in upper], jnp.int32)
    first_cut, second_cut = len(upper) * 7 // 36, len(upper) * 8 // 36
    both = first_cut + second_cut

    order = (0, 1, 2, 5, 3, 6, 4, 7) if paths else tuple(range(row_pairs * col_pairs))
    pair = jnp.asarray(order, jnp.int32)
    turn = pair // (row_pairs * row_pairs)
    own_row = lax.rem(pair, row_pairs)
    own_col = lax.rem(r + ratio - turn, ratio) * row_pairs + lax.rem(pair // row_pairs, row_pairs)
    chosen = domain_tiles[r * row_pairs + own_row, c * col_pairs + own_col]
    corners = [(a, b) for a in range(tiles) for b in range(a, tiles)]
    first = jnp.stack([chosen[:, a] for a, _ in corners], axis=-1)
    second = jnp.stack([chosen[:, b] for _, b in corners], axis=-1)
    flip = (first > second).astype(jnp.int32)
    low, high = jnp.minimum(first, second), jnp.maximum(first, second)
    low, high = low[:, None, :], high[:, None, :]
    number = low * across - low * (low - 1) // 2 + high - low
    vector = jnp.arange(vectors, dtype=jnp.int32)[None, :, None]
    keeps = (c == r // ratio).astype(jnp.int32)
    at_home = (r // 4 == c // 2).astype(jnp.int32)
    source = jnp.where(turn == 0, keeps, jnp.where(pair == row_pairs**2, 0, at_home))
    source = jnp.where(paths, source, 0)
    own = jnp.stack([own_row, own_col, source], axis=-1)
    side = lax.rem(r, 2)

    def target(turn):
        return lambda a, b: (ratio * b + (a + turn) % ratio, a // ratio)

    def sent(turn, first, count, after=()):
        col = lax.rem(r + turn, ratio) * row_pairs
        return sent_pairs(amplitudes, tile_mask, col, first, count, after)

    def table_of(bank, place):
        parts = [jnp.ravel(part) for part in (bank, place, flip, own, tile_mask)]
        starts = [sum(part.size for part in parts[:n]) for n in range(len(parts))]
        return jnp.concatenate(parts).astype(jnp.int32), starts

    square = row_pairs * row_pairs
    if not paths:
        (packed,) = pack(places, cholesky, width, (len(places),))
        banks = [lax.all_gather(packed, "ocol", axis=0, tiled=True)]
        place = vector * len(upper) + number
        bank = jnp.zeros_like(place)
        pieces = [
            ([(lax.ppermute(sent(turn, 0, square), AXES, moves(rows, cols, target(turn))), 0)], square)
            for turn in range(ratio)
        ]
        table, starts = table_of(bank, place)
        choices = ((0,),) * vectors
        return ladder_part(
            amplitudes, tiles, pieces, banks, choices, table, (0, vectors, *starts), None, 0, 0
        )

    crosses = lambda a, b: (a // 4) != (b // 2)
    stays = lambda a, b: not crosses(a, b)
    over_y = moves(rows, cols, lambda a, b: (a, b ^ 2))
    over_x = moves(rows, cols, lambda a, b: (a ^ 1, b))
    over_core = moves(rows, cols, lambda a, b: (a, b ^ 1))
    hop = moves(rows, cols, lambda a, b: (a ^ 1, b ^ 2), crosses)

    finish = moves(rows, cols, lambda a, b: target(1)(a ^ 1, b ^ 2), stays)

    move = lambda value, pairs: lax.ppermute(value, AXES, pairs)
    straight = lambda turn: moves(rows, cols, target(turn), lambda a, b: target(turn)(a, b) != (a, b))
    stay = moves(rows, cols, target(1), stays)
    spot = side * both + jnp.arange(both, dtype=jnp.int32)

    core_near = move(cholesky, over_core)
    other = sent(1, 1, 3)
    hop_all = move(other, hop)
    far_1, far_2, far_3 = pack(
        jnp.concatenate([places[spot], places[2 * both :]]), cholesky, width,
        (first_cut, second_cut, len(upper) - 2 * both), (other,),
    )
    far_1 = move(far_1, over_y)
    kept_1 = sent(0, 0, 2, (other,))
    direct_1 = move(kept_1, straight(0))
    local = move(other, stay)
    kept_2, kept_3, direct_4 = sent(0, 2, 1, (other,)), sent(0, 3, 1, (other,)), sent(1, 0, 1, (other,))
    far_1, far_2, kept_2, kept_3, direct_4 = gate(
        (far_1, far_2, kept_2, kept_3, direct_4), (direct_1, core_near, local)
    )
    far_2 = move(far_2, over_y)
    side_1 = move(far_1, over_x)
    direct_2 = move(kept_2, straight(0))
    hops = [hop_all[n : n + 1] for n in range(3)]
    crossed_1 = move(hops[0], finish)
    core_far_1 = move(far_1, over_core)
    far_2, far_3, kept_3, crossed_2 = gate(
        (far_2, far_3, kept_3, hops[1]),
        (side_1, direct_2, crossed_1, core_far_1),
    )
    far_3 = move(far_3, over_y)
    side_2 = move(far_2, over_x)
    direct_3 = move(kept_3, straight(0))
    crossed_2 = move(crossed_2, finish)
    core_far_2 = move(far_2, over_core)

    is_far = vector >= 2
    theirs = jnp.where(number // both == side, 0, 2)
    inner = lax.rem(number, both)
    second = (inner >= first_cut).astype(jnp.int32)
    last = number >= 2 * both
    bank = jnp.where(is_far, 5 * vector - 8 + jnp.where(last, 4, theirs + second), vector)
    place = jnp.where(
        is_far, jnp.where(last, number - 2 * both, inner - second * first_cut), low * across + high
    )
    table, starts = table_of(*jnp.broadcast_arrays(bank, place))
    choices = ((0,), (1,), (2, 3, 4, 5, 6), (7, 8, 9, 10, 11))
    banks = [cholesky, core_near]

    def part(which, vectors, total, added):
        pieces = [inputs[n] for n in which]
        first = pieces[0][0]
        return ladder_part(
            amplitudes, tiles, [piece[1:] for piece in pieces], banks, choices[:vectors], table,
            (first, len(choices), *starts), total, 2, added,
        )

    inputs = {
        "straight 1": (0, [(direct_1, 0), (kept_1, 0)], 2),
        "straight 2": (2, [(direct_2, 0), (kept_2, 0)], 1),
        "straight 3": (4, [(direct_3, 0), (kept_3, 0)], 1),
        "hop 1": (3, [(crossed_1, 0), (local, 0)], 1),
        "hop 2": (5, [(crossed_2, 0), (local, 1)], 1),
    }
    total = part(["straight 1", "straight 2", "hop 1"], 2, None, 0)
    side_1, side_2, far_3, direct_4, crossed_3 = gate(
        (side_1, side_2, far_3, direct_4, hops[2]),
        (direct_3, crossed_2, core_far_2, total),
    )
    core_far_3 = move(far_3, over_core)
    core_side_1, core_side_2 = move(side_1, over_core), move(side_2, over_core)
    direct_4 = move(direct_4, straight(1))
    crossed_3 = move(crossed_3, finish)
    inputs["straight 4"] = (6, [(direct_4, 0)], 1)
    inputs["hop 3"] = (7, [(crossed_3, 0), (local, 2)], 1)
    banks += [far_1, far_2, side_1, side_2, far_3]
    banks += [core_far_1, core_far_2, core_side_1, core_side_2, core_far_3]
    total = part(["straight 1", "straight 2", "hop 1", "straight 3", "hop 2"], 4, total, 4)
    return part(["straight 4", "hop 3"], 4, total, 0)


def solution(mesh):
    return jax.shard_map(
        functools.partial(shards, mesh.shape["orow"], mesh.shape["ocol"]),
        mesh=mesh,
        in_specs=(
            P("orow", "ocol", None, None),
            P("orow", "ocol", None, None),
            P(),
            P("ocol", None, None),
        ),
        out_specs=P("orow", "ocol", None, None),
        check_vma=False,
    )
```

```python
import functools

import jax
import jax.numpy as jnp
from jax import lax
from jax.experimental import pallas as pl
from jax.experimental.pallas import tpu as pltpu
from jax.sharding import PartitionSpec as P

AXES = ("orow", "ocol")
ANY = pl.BlockSpec(memory_space=pl.ANY)
VMEM = 56 * 2**20
DEEP = 2


def pack_kernel(sizes, width, place_ref, source_ref, *refs):
    held, sems = refs[-2:]
    packed = refs[-2 - len(sizes) : -2]
    loads, stores = [], []
    for part, size in enumerate(sizes):
        for inside in range(size):
            n = len(loads)
            row = pl.multiple_of(place_ref[3 * n + 1] * width, width)
            col = pl.multiple_of(place_ref[3 * n + 2] * width, width)
            loads.append(
                pltpu.make_async_copy(
                    source_ref.at[place_ref[3 * n], pl.ds(row, width), pl.ds(col, width)],
                    held.at[n],
                    sems.at[0, n],
                )
            )
            stores.append(pltpu.make_async_copy(held.at[n], packed[part].at[inside], sems.at[1, n]))
    for load in loads:
        load.start()
    for load, store in zip(loads, stores):
        load.wait()
        store.start()
    for store in stores:
        store.wait()


def pack(places, cholesky, width, sizes, after=()):
    count, dtype = sum(sizes), cholesky.dtype
    return pl.pallas_call(
        functools.partial(pack_kernel, sizes, width),
        out_shape=[jax.ShapeDtypeStruct((size, width, width), dtype) for size in sizes],
        grid_spec=pltpu.PrefetchScalarGridSpec(
            num_scalar_prefetch=1,
            grid=(1,),
            in_specs=[ANY] * (1 + len(after)),
            out_specs=[ANY] * len(sizes),
            scratch_shapes=[
                pltpu.VMEM((count, width, width), dtype),
                pltpu.SemaphoreType.DMA((2, count)),
            ],
        ),
        compiler_params=pltpu.CompilerParams(vmem_limit_bytes=VMEM),
        cost_estimate=pl.CostEstimate(
            flops=0, bytes_accessed=count * width * width // 16, transcendentals=0
        ),
        name="pack_tiles",
    )(places.reshape(-1), cholesky, *after)


def keep_tiles(source, mask_ref, base, tiles, width, store):
    for a in range(tiles):
        for b in range(tiles):
            rows, cols = slice(a * width, (a + 1) * width), slice(b * width, (b + 1) * width)
            block = source[rows, cols]
            store(rows, cols, block * mask_ref[base + a * tiles + b].astype(block.dtype))


def send_kernel(tiles, width, rows, col_pairs, first, *refs):
    start_ref, mask_ref, amps_ref = refs[:3]
    out_ref = refs[-1]
    pair = first + pl.program_id(0)
    base = ((pair // rows) * col_pairs + start_ref[0] + lax.rem(pair, rows)) * tiles * tiles

    def store(rows, cols, value):
        out_ref[0, rows, cols] = value

    keep_tiles(amps_ref.at[0, 0], mask_ref, base, tiles, width, store)


def sent_pairs(amplitudes, tile_mask, col, first, count, after=()):
    rows, col_pairs, depth, _ = amplitudes.shape
    tiles = tile_mask.shape[-1]

    def source(i, start, mask):
        return (first + i) // rows, start[0] + lax.rem(first + i, rows), 0, 0

    return pl.pallas_call(
        functools.partial(send_kernel, tiles, depth // tiles, rows, col_pairs, first),
        out_shape=jax.ShapeDtypeStruct((count, depth, depth), amplitudes.dtype),
        grid_spec=pltpu.PrefetchScalarGridSpec(
            num_scalar_prefetch=2,
            grid=(count,),
            in_specs=[pl.BlockSpec((1, 1, depth, depth), source)] + [ANY] * len(after),
            out_specs=pl.BlockSpec((1, depth, depth), lambda i, start, mask: (i, 0, 0)),
        ),
        compiler_params=pltpu.CompilerParams(vmem_limit_bytes=VMEM),
        cost_estimate=pl.CostEstimate(
            flops=0, bytes_accessed=count * depth * depth // 16, transcendentals=0
        ),
        name="sent_pairs",
    )(col.reshape(1).astype(jnp.int32), tile_mask.reshape(-1), amplitudes, *after)


class View:
    def __init__(self, ref, start):
        self.ref, self.start = ref, start

    def __getitem__(self, index):
        return self.ref[self.start + index]


def ladder_kernel(tiles, width, counts, number, choices, early, added, col_pairs, starts, *refs):
    table_ref, amps_ref = refs[:2]
    base_pair, stride = starts[:2]
    slots = [(a, b) for a in range(tiles) for b in range(a, tiles)]
    bank_ref, place_ref = (View(table_ref, start + base_pair * stride * len(slots)) for start in starts[2:4])
    flip_ref = View(table_ref, starts[4] + base_pair * len(slots))
    own_ref, mask_ref = View(table_ref, starts[5] + 3 * base_pair), View(table_ref, starts[6])
    pieces, at = [], 2
    for firsts, pairs in counts:
        pieces.append((refs[at : at + len(firsts)], firsts, pairs))
        at += len(firsts)
    banks = refs[at : at + number]
    total_ref = refs[at + number] if added else None
    out_ref, factor, weighted, partner, sems, partner_sems = refs[-6:]
    pair, steps = pl.program_id(0), pl.num_programs(0)
    vectors = len(choices)

    def corner(index):
        return pl.ds(pl.multiple_of(index * width, width), width)

    def tile_of(bank, place):
        if bank.shape[-1] == width:
            return bank.at[place]
        across = bank.shape[-1] // width
        return bank.at[0, corner(place // across), corner(lax.rem(place, across))]

    def ends(which, pair):
        a, b = slots[which]
        if a == b:
            return a, b
        flip = flip_ref[pair * len(slots) + which]
        return a + flip * (b - a), b + flip * (a - b)

    def fetch(pair, slot, chosen):
        for vector in chosen:
            for which in range(len(slots)):
                entry = (pair * stride + vector) * len(slots) + which
                row, col = ends(which, pair)

                def begin(n):
                    pltpu.make_async_copy(
                        tile_of(banks[n], place_ref[entry]),
                        factor.at[slot, vector, corner(row), corner(col)],
                        sems.at[slot, vector, which],
                    ).start()

                if len(choices[vector]) == 1:
                    begin(choices[vector][0])
                else:
                    for n in choices[vector]:
                        pl.when(bank_ref[entry] == n)(functools.partial(begin, n))

    def fetch_partner(pair, slot):
        first = 0
        for arrays, firsts, pairs in pieces:
            for m, (array, start) in enumerate(zip(arrays, firsts)):
                here = (pair >= first) & (pair < first + pairs)
                if len(arrays) > 1:
                    here &= own_ref[3 * pair + 2] == m

                @pl.when(here)
                def _():
                    pltpu.make_async_copy(
                        array.at[start + pair - first], partner.at[slot], partner_sems.at[slot]
                    ).start()
            first += pairs

    def fetch_all(pair, slot):
        fetch_partner(pair, slot)
        if added:
            pl.when(pair >= added)(lambda: fetch(pair, slot, range(early)))
        fetch(pair, slot, range(early if added else 0, vectors))

    slot = lax.rem(pair, DEEP)

    @pl.when(pair == 0)
    def _():
        fetch_all(pair, slot)

    def fetch_next():
        @pl.when(pair + 1 < steps)
        def _():
            fetch_all(pair + 1, 1 - slot)

    def store(rows, cols, value):
        weighted[rows, cols] = value

    base = (own_ref[3 * pair] * col_pairs + own_ref[3 * pair + 1]) * tiles * tiles
    keep_tiles(amps_ref.at[0, 0], mask_ref, base, tiles, width, store)
    pltpu.make_async_copy(
        pieces[0][0][0].at[0], partner.at[slot], partner_sems.at[slot]
    ).wait()

    def arrive(chosen):
        for vector in chosen:
            for which in range(len(slots)):
                row, col = ends(which, pair)
                pltpu.make_async_copy(
                    tile_of(banks[0], 0),
                    factor.at[slot, vector, corner(row), corner(col)],
                    sems.at[slot, vector, which],
                ).wait()
                if slots[which][0] != slots[which][1]:
                    factor[slot, vector, corner(col), corner(row)] = factor[
                        slot, vector, corner(row), corner(col)
                    ].T

    def products(chosen):
        total = None
        for vector in chosen:
            whole = factor[slot, vector]
            inner = jnp.dot(whole, weighted[...], preferred_element_type=jnp.float32)
            inner += lax.dot_general(
                whole, partner[slot], (((1,), (1,)), ((), ())), preferred_element_type=jnp.float32
            )
            term = jnp.dot(inner.astype(jnp.bfloat16), whole, preferred_element_type=jnp.float32)
            total = term if total is None else total + term
        return total

    if not added:
        arrive(range(vectors))
        fetch_next()
        out_ref[0, 0] = products(range(vectors))
        return

    @pl.when(pair < added)
    def _():
        arrive(range(early, vectors))
        fetch_next()
        out_ref[0, 0] = total_ref[0, 0] + products(range(early, vectors))

    @pl.when(pair >= added)
    def _():
        arrive(range(vectors))
        fetch_next()
        out_ref[0, 0] = products(range(vectors))


def ladder_part(amplitudes, tiles, pieces, banks, choices, table, starts, total, early, added):
    pairs, vectors = sum(count for _, count in pieces), len(choices)
    slots = tiles * (tiles + 1) // 2
    col_pairs, depth = amplitudes.shape[1:3]
    width = depth // tiles
    block = (1, 1, depth, depth)

    def own_map(pair, table):
        own = starts[5] + 3 * (starts[0] + pair)
        return table[own], table[own + 1], 0, 0

    def total_map(pair, table):
        return own_map(jnp.minimum(pair, added - 1), table)

    in_specs, operands, counts = [pl.BlockSpec(block, own_map)], [amplitudes], []
    for arrays, count in pieces:
        for array, _ in arrays:
            in_specs.append(ANY)
            operands.append(array)
        counts.append((tuple(start for _, start in arrays), count))
    in_specs += [ANY] * len(banks)
    operands += banks
    aliases = {}
    if total is not None:
        aliases = {1 + len(operands): 0}
        operands.append(total)
        in_specs.append(pl.BlockSpec(block, total_map) if added else ANY)
    flops = 6 * pairs * vectors * depth**3
    moved = pairs * (depth * depth * 8 + vectors * slots * width * width * 2)
    return pl.pallas_call(
        functools.partial(
            ladder_kernel, tiles, width, tuple(counts), len(banks), choices, early, added, col_pairs,
            starts,
        ),
        out_shape=jax.ShapeDtypeStruct(amplitudes.shape, jnp.float32),
        grid_spec=pltpu.PrefetchScalarGridSpec(
            num_scalar_prefetch=1,
            grid=(pairs,),
            in_specs=in_specs,
            out_specs=pl.BlockSpec(block, own_map),
            scratch_shapes=[
                pltpu.VMEM((DEEP, vectors, depth, depth), jnp.bfloat16),
                pltpu.VMEM((depth, depth), jnp.bfloat16),
                pltpu.VMEM((DEEP, depth, depth), jnp.bfloat16),
                pltpu.SemaphoreType.DMA((DEEP, vectors, slots)),
                pltpu.SemaphoreType.DMA((DEEP,)),
            ],
        ),
        input_output_aliases=aliases,
        compiler_params=pltpu.CompilerParams(
            dimension_semantics=("arbitrary",), vmem_limit_bytes=VMEM
        ),
        cost_estimate=pl.CostEstimate(flops=flops // 64, bytes_accessed=moved // 64, transcendentals=0),
        name="ladder_part",
    )(table, *operands)


def gate_kernel(*refs):
    pass


def gate(values, after):
    return pl.pallas_call(
        gate_kernel,
        out_shape=[jax.ShapeDtypeStruct(value.shape, value.dtype) for value in values],
        in_specs=[ANY] * (len(values) + len(after)),
        out_specs=[ANY] * len(values),
        input_output_aliases={n: n for n in range(len(values))},
        compiler_params=pltpu.CompilerParams(vmem_limit_bytes=VMEM),
        cost_estimate=pl.CostEstimate(flops=0, bytes_accessed=0, transcendentals=0),
        name="gate",
    )(*values, *after)


def moves(rows, cols, change, chosen=lambda r, c: True):
    pairs = []
    for r in range(rows):
        for c in range(cols):
            if chosen(r, c):
                to_row, to_col = change(r, c)
                pairs.append((r * cols + c, to_row * cols + to_col))
    return pairs


def shards(rows, cols, amplitudes, tile_mask, domain_tiles, cholesky):
    row_pairs, col_pairs, depth, _ = amplitudes.shape
    tiles = domain_tiles.shape[-1]
    width = depth // tiles
    held = cholesky.shape[0]
    across = cholesky.shape[1] // width
    vectors = held * cols
    ratio = col_pairs // row_pairs
    r, c = lax.axis_index("orow"), lax.axis_index("ocol")

    paths = rows == 8 and cols == 4 and row_pairs == 2 and held == 1

    upper = [(s, t) for s in range(across) for t in range(s, across)]
    places = jnp.asarray([[q, s, t] for q in range(held) for s, t in upper], jnp.int32)
    first_cut, second_cut = len(upper) * 7 // 36, len(upper) * 8 // 36
    both = first_cut + second_cut

    order = (0, 1, 2, 5, 3, 6, 4, 7) if paths else tuple(range(row_pairs * col_pairs))
    pair = jnp.asarray(order, jnp.int32)
    turn = pair // (row_pairs * row_pairs)
    own_row = lax.rem(pair, row_pairs)
    own_col = lax.rem(r + ratio - turn, ratio) * row_pairs + lax.rem(pair // row_pairs, row_pairs)
    chosen = domain_tiles[r * row_pairs + own_row, c * col_pairs + own_col]
    corners = [(a, b) for a in range(tiles) for b in range(a, tiles)]
    first = jnp.stack([chosen[:, a] for a, _ in corners], axis=-1)
    second = jnp.stack([chosen[:, b] for _, b in corners], axis=-1)
    flip = (first > second).astype(jnp.int32)
    low, high = jnp.minimum(first, second), jnp.maximum(first, second)
    low, high = low[:, None, :], high[:, None, :]
    number = low * across - low * (low - 1) // 2 + high - low
    vector = jnp.arange(vectors, dtype=jnp.int32)[None, :, None]
    keeps = (c == r // ratio).astype(jnp.int32)
    at_home = (r // 4 == c // 2).astype(jnp.int32)
    source = jnp.where(turn == 0, keeps, jnp.where(pair == row_pairs**2, 0, at_home))
    source = jnp.where(paths, source, 0)
    own = jnp.stack([own_row, own_col, source], axis=-1)
    side = lax.rem(r, 2)

    def target(turn):
        return lambda a, b: (ratio * b + (a + turn) % ratio, a // ratio)

    def sent(turn, first, count, after=()):
        col = lax.rem(r + turn, ratio) * row_pairs
        return sent_pairs(amplitudes, tile_mask, col, first, count, after)

    def table_of(bank, place):
        parts = [jnp.ravel(part) for part in (bank, place, flip, own, tile_mask)]
        starts = [sum(part.size for part in parts[:n]) for n in range(len(parts))]
        return jnp.concatenate(parts).astype(jnp.int32), starts

    square = row_pairs * row_pairs
    if not paths:
        (packed,) = pack(places, cholesky, width, (len(places),))
        banks = [lax.all_gather(packed, "ocol", axis=0, tiled=True)]
        place = vector * len(upper) + number
        bank = jnp.zeros_like(place)
        pieces = [
            ([(lax.ppermute(sent(turn, 0, square), AXES, moves(rows, cols, target(turn))), 0)], square)
            for turn in range(ratio)
        ]
        table, starts = table_of(bank, place)
        choices = ((0,),) * vectors
        return ladder_part(
            amplitudes, tiles, pieces, banks, choices, table, (0, vectors, *starts), None, 0, 0
        )

    crosses = lambda a, b: (a // 4) != (b // 2)
    stays = lambda a, b: not crosses(a, b)
    over_y = moves(rows, cols, lambda a, b: (a, b ^ 2))
    over_x = moves(rows, cols, lambda a, b: (a ^ 1, b))
    over_core = moves(rows, cols, lambda a, b: (a, b ^ 1))
    hop = moves(rows, cols, lambda a, b: (a ^ 1, b ^ 2), crosses)

    finish = moves(rows, cols, lambda a, b: target(1)(a ^ 1, b ^ 2), stays)

    move = lambda value, pairs: lax.ppermute(value, AXES, pairs)
    straight = lambda turn: moves(rows, cols, target(turn), lambda a, b: target(turn)(a, b) != (a, b))
    stay = moves(rows, cols, target(1), stays)
    spot = side * both + jnp.arange(both, dtype=jnp.int32)

    core_near = move(cholesky, over_core)
    other = sent(1, 1, 3)
    hop_all = move(other, hop)
    far_1, far_2, far_3 = pack(
        jnp.concatenate([places[spot], places[2 * both :]]), cholesky, width,
        (first_cut, second_cut, len(upper) - 2 * both), (other,),
    )
    far_1 = move(far_1, over_y)
    kept_1 = sent(0, 0, 2, (other,))
    direct_1 = move(kept_1, straight(0))
    local = move(other, stay)
    kept_2, kept_3, direct_4 = sent(0, 2, 1, (other,)), sent(0, 3, 1, (other,)), sent(1, 0, 1, (other,))
    far_1, far_2, kept_2, kept_3, direct_4 = gate(
        (far_1, far_2, kept_2, kept_3, direct_4), (direct_1, core_near)
    )
    far_2 = move(far_2, over_y)
    side_1 = move(far_1, over_x)
    direct_2 = move(kept_2, straight(0))
    hops = [hop_all[n : n + 1] for n in range(3)]
    crossed_1 = move(hops[0], finish)
    core_far_1 = move(far_1, over_core)
    far_2, far_3, kept_3, crossed_2 = gate(
        (far_2, far_3, kept_3, hops[1]),
        (side_1, direct_2, crossed_1, core_far_1, local),
    )
    far_3 = move(far_3, over_y)
    side_2 = move(far_2, over_x)
    direct_3 = move(kept_3, straight(0))
    crossed_2 = move(crossed_2, finish)
    core_far_2 = move(far_2, over_core)

    is_far = vector >= 2
    theirs = jnp.where(number // both == side, 0, 2)
    inner = lax.rem(number, both)
    second = (inner >= first_cut).astype(jnp.int32)
    last = number >= 2 * both
    bank = jnp.where(is_far, 5 * vector - 8 + jnp.where(last, 4, theirs + second), vector)
    place = jnp.where(
        is_far, jnp.where(last, number - 2 * both, inner - second * first_cut), low * across + high
    )
    table, starts = table_of(*jnp.broadcast_arrays(bank, place))
    choices = ((0,), (1,), (2, 3, 4, 5, 6), (7, 8, 9, 10, 11))
    banks = [cholesky, core_near]

    def part(which, vectors, total, added):
        pieces = [inputs[n] for n in which]
        first = pieces[0][0]
        return ladder_part(
            amplitudes, tiles, [piece[1:] for piece in pieces], banks, choices[:vectors], table,
            (first, len(choices), *starts), total, 2, added,
        )

    inputs = {
        "straight 1": (0, [(direct_1, 0), (kept_1, 0)], 2),
        "straight 2": (2, [(direct_2, 0), (kept_2, 0)], 1),
        "straight 3": (4, [(direct_3, 0), (kept_3, 0)], 1),
        "hop 1": (3, [(crossed_1, 0), (local, 0)], 1),
        "hop 2": (5, [(crossed_2, 0), (local, 1)], 1),
    }
    total = part(["straight 1", "straight 2", "hop 1"], 2, None, 0)
    side_1, side_2, far_3, direct_4, crossed_3 = gate(
        (side_1, side_2, far_3, direct_4, hops[2]),
        (direct_3, crossed_2, core_far_2, total),
    )
    core_far_3 = move(far_3, over_core)
    core_side_1, core_side_2 = move(side_1, over_core), move(side_2, over_core)
    direct_4 = move(direct_4, straight(1))
    crossed_3 = move(crossed_3, finish)
    inputs["straight 4"] = (6, [(direct_4, 0)], 1)
    inputs["hop 3"] = (7, [(crossed_3, 0), (local, 2)], 1)
    banks += [far_1, far_2, side_1, side_2, far_3]
    banks += [core_far_1, core_far_2, core_side_1, core_side_2, core_far_3]
    total = part(["straight 1", "straight 2", "hop 1", "straight 3", "hop 2"], 4, total, 4)
    return part(["straight 4", "hop 3"], 4, total, 0)


def solution(mesh):
    return jax.shard_map(
        functools.partial(shards, mesh.shape["orow"], mesh.shape["ocol"]),
        mesh=mesh,
        in_specs=(
            P("orow", "ocol", None, None),
            P("orow", "ocol", None, None),
            P(),
            P("ocol", None, None),
        ),
        out_specs=P("orow", "ocol", None, None),
        check_vma=False,
    )
```

```python
import functools

import jax
import jax.numpy as jnp
from jax import lax
from jax.experimental import pallas as pl
from jax.experimental.pallas import tpu as pltpu
from jax.sharding import PartitionSpec as P

AXES = ("orow", "ocol")
ANY = pl.BlockSpec(memory_space=pl.ANY)
VMEM = 56 * 2**20
DEEP = 2


def pack_kernel(sizes, width, place_ref, source_ref, *refs):
    held, sems = refs[-2:]
    packed = refs[-2 - len(sizes) : -2]
    loads, stores = [], []
    for part, size in enumerate(sizes):
        for inside in range(size):
            n = len(loads)
            row = pl.multiple_of(place_ref[3 * n + 1] * width, width)
            col = pl.multiple_of(place_ref[3 * n + 2] * width, width)
            loads.append(
                pltpu.make_async_copy(
                    source_ref.at[place_ref[3 * n], pl.ds(row, width), pl.ds(col, width)],
                    held.at[n],
                    sems.at[0, n],
                )
            )
            stores.append(pltpu.make_async_copy(held.at[n], packed[part].at[inside], sems.at[1, n]))
    for load in loads:
        load.start()
    for load, store in zip(loads, stores):
        load.wait()
        store.start()
    for store in stores:
        store.wait()


def pack(places, cholesky, width, sizes, after=()):
    count, dtype = sum(sizes), cholesky.dtype
    return pl.pallas_call(
        functools.partial(pack_kernel, sizes, width),
        out_shape=[jax.ShapeDtypeStruct((size, width, width), dtype) for size in sizes],
        grid_spec=pltpu.PrefetchScalarGridSpec(
            num_scalar_prefetch=1,
            grid=(1,),
            in_specs=[ANY] * (1 + len(after)),
            out_specs=[ANY] * len(sizes),
            scratch_shapes=[
                pltpu.VMEM((count, width, width), dtype),
                pltpu.SemaphoreType.DMA((2, count)),
            ],
        ),
        compiler_params=pltpu.CompilerParams(vmem_limit_bytes=VMEM),
        cost_estimate=pl.CostEstimate(
            flops=0, bytes_accessed=count * width * width // 16, transcendentals=0
        ),
        name="pack_tiles",
    )(places.reshape(-1), cholesky, *after)


def keep_tiles(source, mask_ref, base, tiles, width, store):
    for a in range(tiles):
        for b in range(tiles):
            rows, cols = slice(a * width, (a + 1) * width), slice(b * width, (b + 1) * width)
            block = source[rows, cols]
            store(rows, cols, block * mask_ref[base + a * tiles + b].astype(block.dtype))


def send_kernel(tiles, width, rows, col_pairs, first, *refs):
    start_ref, mask_ref, amps_ref = refs[:3]
    out_ref = refs[-1]
    pair = first + pl.program_id(0)
    base = ((pair // rows) * col_pairs + start_ref[0] + lax.rem(pair, rows)) * tiles * tiles

    def store(rows, cols, value):
        out_ref[0, rows, cols] = value

    keep_tiles(amps_ref.at[0, 0], mask_ref, base, tiles, width, store)


def sent_pairs(amplitudes, tile_mask, col, first, count, after=()):
    rows, col_pairs, depth, _ = amplitudes.shape
    tiles = tile_mask.shape[-1]

    def source(i, start, mask):
        return (first + i) // rows, start[0] + lax.rem(first + i, rows), 0, 0

    return pl.pallas_call(
        functools.partial(send_kernel, tiles, depth // tiles, rows, col_pairs, first),
        out_shape=jax.ShapeDtypeStruct((count, depth, depth), amplitudes.dtype),
        grid_spec=pltpu.PrefetchScalarGridSpec(
            num_scalar_prefetch=2,
            grid=(count,),
            in_specs=[pl.BlockSpec((1, 1, depth, depth), source)] + [ANY] * len(after),
            out_specs=pl.BlockSpec((1, depth, depth), lambda i, start, mask: (i, 0, 0)),
        ),
        compiler_params=pltpu.CompilerParams(vmem_limit_bytes=VMEM),
        cost_estimate=pl.CostEstimate(
            flops=0, bytes_accessed=count * depth * depth // 16, transcendentals=0
        ),
        name="sent_pairs",
    )(col.reshape(1).astype(jnp.int32), tile_mask.reshape(-1), amplitudes, *after)


class View:
    def __init__(self, ref, start):
        self.ref, self.start = ref, start

    def __getitem__(self, index):
        return self.ref[self.start + index]


def ladder_kernel(tiles, width, counts, number, choices, early, added, col_pairs, starts, *refs):
    table_ref, amps_ref = refs[:2]
    base_pair, stride = starts[:2]
    slots = [(a, b) for a in range(tiles) for b in range(a, tiles)]
    bank_ref, place_ref = (View(table_ref, start + base_pair * stride * len(slots)) for start in starts[2:4])
    flip_ref = View(table_ref, starts[4] + base_pair * len(slots))
    own_ref, mask_ref = View(table_ref, starts[5] + 3 * base_pair), View(table_ref, starts[6])
    pieces, at = [], 2
    for firsts, pairs in counts:
        pieces.append((refs[at : at + len(firsts)], firsts, pairs))
        at += len(firsts)
    banks = refs[at : at + number]
    total_ref = refs[at + number] if added else None
    out_ref, factor, weighted, partner, mine, sums, sems, block_sems = refs[-8:]
    pair, steps = pl.program_id(0), pl.num_programs(0)
    vectors = len(choices)

    def corner(index):
        return pl.ds(pl.multiple_of(index * width, width), width)

    def tile_of(bank, place):
        if bank.shape[-1] == width:
            return bank.at[place]
        across = bank.shape[-1] // width
        return bank.at[0, corner(place // across), corner(lax.rem(place, across))]

    def ends(which, pair):
        a, b = slots[which]
        if a == b:
            return a, b
        flip = flip_ref[pair * len(slots) + which]
        return a + flip * (b - a), b + flip * (a - b)

    def fetch(pair, slot, chosen):
        for vector in chosen:
            for which in range(len(slots)):
                entry = (pair * stride + vector) * len(slots) + which
                row, col = ends(which, pair)

                def begin(n):
                    pltpu.make_async_copy(
                        tile_of(banks[n], place_ref[entry]),
                        factor.at[slot, vector, corner(row), corner(col)],
                        sems.at[slot, vector, which],
                    ).start()

                if len(choices[vector]) == 1:
                    begin(choices[vector][0])
                else:
                    for n in choices[vector]:
                        pl.when(bank_ref[entry] == n)(functools.partial(begin, n))

    def fetch_partner(pair, slot):
        first = 0
        for arrays, firsts, pairs in pieces:
            for m, (array, start) in enumerate(zip(arrays, firsts)):
                here = (pair >= first) & (pair < first + pairs)
                if len(arrays) > 1:
                    here &= own_ref[3 * pair + 2] == m

                @pl.when(here)
                def _():
                    pltpu.make_async_copy(
                        array.at[start + pair - first], partner.at[slot], block_sems.at[slot, 0]
                    ).start()
            first += pairs

    def fetch_all(pair, slot):
        row, col = own_ref[3 * pair], own_ref[3 * pair + 1]
        pltpu.make_async_copy(amps_ref.at[row, col], mine.at[slot], block_sems.at[slot, 1]).start()
        fetch_partner(pair, slot)
        if added:
            pl.when(pair >= added)(lambda: fetch(pair, slot, range(early)))
        fetch(pair, slot, range(early if added else 0, vectors))
        if added:
            @pl.when(pair < added)
            def _():
                pltpu.make_async_copy(
                    total_ref.at[row, col], sums.at[slot], block_sems.at[slot, 2]
                ).start()

    slot = lax.rem(pair, DEEP)

    @pl.when(pair == 0)
    def _():
        fetch_all(pair, slot)

    def fetch_next():
        @pl.when(pair + 1 < steps)
        def _():
            fetch_all(pair + 1, 1 - slot)

    def store(rows, cols, value):
        weighted[rows, cols] = value

    base = (own_ref[3 * pair] * col_pairs + own_ref[3 * pair + 1]) * tiles * tiles
    pltpu.make_async_copy(amps_ref.at[0, 0], mine.at[slot], block_sems.at[slot, 1]).wait()
    keep_tiles(mine.at[slot], mask_ref, base, tiles, width, store)
    pltpu.make_async_copy(
        pieces[0][0][0].at[0], partner.at[slot], block_sems.at[slot, 0]
    ).wait()

    def arrive(chosen):
        for vector in chosen:
            for which in range(len(slots)):
                row, col = ends(which, pair)
                pltpu.make_async_copy(
                    tile_of(banks[0], 0),
                    factor.at[slot, vector, corner(row), corner(col)],
                    sems.at[slot, vector, which],
                ).wait()
                if slots[which][0] != slots[which][1]:
                    factor[slot, vector, corner(col), corner(row)] = factor[
                        slot, vector, corner(row), corner(col)
                    ].T

    def products(chosen):
        total = None
        for vector in chosen:
            whole = factor[slot, vector]
            inner = jnp.dot(whole, weighted[...], preferred_element_type=jnp.float32)
            inner += lax.dot_general(
                whole, partner[slot], (((1,), (1,)), ((), ())), preferred_element_type=jnp.float32
            )
            term = jnp.dot(inner.astype(jnp.bfloat16), whole, preferred_element_type=jnp.float32)
            total = term if total is None else total + term
        return total

    if not added:
        arrive(range(vectors))
        fetch_next()
        out_ref[0, 0] = products(range(vectors))
        return

    @pl.when(pair < added)
    def _():
        arrive(range(early, vectors))
        fetch_next()
        pltpu.make_async_copy(total_ref.at[0, 0], sums.at[slot], block_sems.at[slot, 2]).wait()
        out_ref[0, 0] = sums[slot] + products(range(early, vectors))

    @pl.when(pair >= added)
    def _():
        arrive(range(vectors))
        fetch_next()
        out_ref[0, 0] = products(range(vectors))


def ladder_part(amplitudes, tiles, pieces, banks, choices, table, starts, total, early, added):
    pairs, vectors = sum(count for _, count in pieces), len(choices)
    slots = tiles * (tiles + 1) // 2
    col_pairs, depth = amplitudes.shape[1:3]
    width = depth // tiles
    block = (1, 1, depth, depth)

    def own_map(pair, table):
        own = starts[5] + 3 * (starts[0] + pair)
        return table[own], table[own + 1], 0, 0

    in_specs, operands, counts = [ANY], [amplitudes], []
    for arrays, count in pieces:
        for array, _ in arrays:
            in_specs.append(ANY)
            operands.append(array)
        counts.append((tuple(start for _, start in arrays), count))
    in_specs += [ANY] * len(banks)
    operands += banks
    aliases = {}
    if total is not None:
        aliases = {1 + len(operands): 0}
        operands.append(total)
        in_specs.append(ANY)
    flops = 6 * pairs * vectors * depth**3
    moved = pairs * (depth * depth * 8 + vectors * slots * width * width * 2)
    return pl.pallas_call(
        functools.partial(
            ladder_kernel, tiles, width, tuple(counts), len(banks), choices, early, added, col_pairs,
            starts,
        ),
        out_shape=jax.ShapeDtypeStruct(amplitudes.shape, jnp.float32),
        grid_spec=pltpu.PrefetchScalarGridSpec(
            num_scalar_prefetch=1,
            grid=(pairs,),
            in_specs=in_specs,
            out_specs=pl.BlockSpec(block, own_map),
            scratch_shapes=[
                pltpu.VMEM((DEEP, vectors, depth, depth), jnp.bfloat16),
                pltpu.VMEM((depth, depth), jnp.bfloat16),
                pltpu.VMEM((DEEP, depth, depth), jnp.bfloat16),
                pltpu.VMEM((DEEP, depth, depth), jnp.bfloat16),
                pltpu.VMEM((DEEP if added else 1, depth, depth), jnp.float32),
                pltpu.SemaphoreType.DMA((DEEP, vectors, slots)),
                pltpu.SemaphoreType.DMA((DEEP, 3)),
            ],
        ),
        input_output_aliases=aliases,
        compiler_params=pltpu.CompilerParams(
            dimension_semantics=("arbitrary",), vmem_limit_bytes=VMEM
        ),
        cost_estimate=pl.CostEstimate(flops=flops // 64, bytes_accessed=moved // 64, transcendentals=0),
        name="ladder_part",
    )(table, *operands)


def gate_kernel(*refs):
    pass


def gate(values, after):
    return pl.pallas_call(
        gate_kernel,
        out_shape=[jax.ShapeDtypeStruct(value.shape, value.dtype) for value in values],
        in_specs=[ANY] * (len(values) + len(after)),
        out_specs=[ANY] * len(values),
        input_output_aliases={n: n for n in range(len(values))},
        compiler_params=pltpu.CompilerParams(vmem_limit_bytes=VMEM),
        cost_estimate=pl.CostEstimate(flops=0, bytes_accessed=0, transcendentals=0),
        name="gate",
    )(*values, *after)


def moves(rows, cols, change, chosen=lambda r, c: True):
    pairs = []
    for r in range(rows):
        for c in range(cols):
            if chosen(r, c):
                to_row, to_col = change(r, c)
                pairs.append((r * cols + c, to_row * cols + to_col))
    return pairs


def shards(rows, cols, amplitudes, tile_mask, domain_tiles, cholesky):
    row_pairs, col_pairs, depth, _ = amplitudes.shape
    tiles = domain_tiles.shape[-1]
    width = depth // tiles
    held = cholesky.shape[0]
    across = cholesky.shape[1] // width
    vectors = held * cols
    ratio = col_pairs // row_pairs
    r, c = lax.axis_index("orow"), lax.axis_index("ocol")

    paths = rows == 8 and cols == 4 and row_pairs == 2 and held == 1

    upper = [(s, t) for s in range(across) for t in range(s, across)]
    places = jnp.asarray([[q, s, t] for q in range(held) for s, t in upper], jnp.int32)
    first_cut, second_cut = len(upper) * 7 // 36, len(upper) * 8 // 36
    both = first_cut + second_cut

    order = (0, 1, 2, 5, 3, 6, 4, 7) if paths else tuple(range(row_pairs * col_pairs))
    pair = jnp.asarray(order, jnp.int32)
    turn = pair // (row_pairs * row_pairs)
    own_row = lax.rem(pair, row_pairs)
    own_col = lax.rem(r + ratio - turn, ratio) * row_pairs + lax.rem(pair // row_pairs, row_pairs)
    chosen = domain_tiles[r * row_pairs + own_row, c * col_pairs + own_col]
    corners = [(a, b) for a in range(tiles) for b in range(a, tiles)]
    first = jnp.stack([chosen[:, a] for a, _ in corners], axis=-1)
    second = jnp.stack([chosen[:, b] for _, b in corners], axis=-1)
    flip = (first > second).astype(jnp.int32)
    low, high = jnp.minimum(first, second), jnp.maximum(first, second)
    low, high = low[:, None, :], high[:, None, :]
    number = low * across - low * (low - 1) // 2 + high - low
    vector = jnp.arange(vectors, dtype=jnp.int32)[None, :, None]
    keeps = (c == r // ratio).astype(jnp.int32)
    at_home = (r // 4 == c // 2).astype(jnp.int32)
    source = jnp.where(turn == 0, keeps, jnp.where(pair == row_pairs**2, 0, at_home))
    source = jnp.where(paths, source, 0)
    own = jnp.stack([own_row, own_col, source], axis=-1)
    side = lax.rem(r, 2)

    def target(turn):
        return lambda a, b: (ratio * b + (a + turn) % ratio, a // ratio)

    def sent(turn, first, count, after=()):
        col = lax.rem(r + turn, ratio) * row_pairs
        return sent_pairs(amplitudes, tile_mask, col, first, count, after)

    def table_of(bank, place):
        parts = [jnp.ravel(part) for part in (bank, place, flip, own, tile_mask)]
        starts = [sum(part.size for part in parts[:n]) for n in range(len(parts))]
        return jnp.concatenate(parts).astype(jnp.int32), starts

    square = row_pairs * row_pairs
    if not paths:
        (packed,) = pack(places, cholesky, width, (len(places),))
        banks = [lax.all_gather(packed, "ocol", axis=0, tiled=True)]
        place = vector * len(upper) + number
        bank = jnp.zeros_like(place)
        pieces = [
            ([(lax.ppermute(sent(turn, 0, square), AXES, moves(rows, cols, target(turn))), 0)], square)
            for turn in range(ratio)
        ]
        table, starts = table_of(bank, place)
        choices = ((0,),) * vectors
        return ladder_part(
            amplitudes, tiles, pieces, banks, choices, table, (0, vectors, *starts), None, 0, 0
        )

    crosses = lambda a, b: (a // 4) != (b // 2)
    stays = lambda a, b: not crosses(a, b)
    over_y = moves(rows, cols, lambda a, b: (a, b ^ 2))
    over_x = moves(rows, cols, lambda a, b: (a ^ 1, b))
    over_core = moves(rows, cols, lambda a, b: (a, b ^ 1))
    hop = moves(rows, cols, lambda a, b: (a ^ 1, b ^ 2), crosses)

    finish = moves(rows, cols, lambda a, b: target(1)(a ^ 1, b ^ 2), stays)

    move = lambda value, pairs: lax.ppermute(value, AXES, pairs)
    straight = lambda turn: moves(rows, cols, target(turn), lambda a, b: target(turn)(a, b) != (a, b))
    stay = moves(rows, cols, target(1), stays)
    spot = side * both + jnp.arange(both, dtype=jnp.int32)

    core_near = move(cholesky, over_core)
    other = sent(1, 1, 3)
    hop_all = move(other, hop)
    far_1, far_2, far_3 = pack(
        jnp.concatenate([places[spot], places[2 * both :]]), cholesky, width,
        (first_cut, second_cut, len(upper) - 2 * both), (other,),
    )
    far_1 = move(far_1, over_y)
    kept_1 = sent(0, 0, 2, (other,))
    direct_1 = move(kept_1, straight(0))
    local = move(other, stay)
    kept_2, kept_3, direct_4 = sent(0, 2, 1, (other,)), sent(0, 3, 1, (other,)), sent(1, 0, 1, (other,))
    far_1, far_2, kept_2, kept_3, direct_4 = gate(
        (far_1, far_2, kept_2, kept_3, direct_4), (direct_1, core_near)
    )
    far_2 = move(far_2, over_y)
    side_1 = move(far_1, over_x)
    direct_2 = move(kept_2, straight(0))
    hops = [hop_all[n : n + 1] for n in range(3)]
    crossed_1 = move(hops[0], finish)
    core_far_1 = move(far_1, over_core)
    far_2, far_3, kept_3, crossed_2 = gate(
        (far_2, far_3, kept_3, hops[1]),
        (side_1, direct_2, crossed_1, core_far_1, local),
    )
    far_3 = move(far_3, over_y)
    side_2 = move(far_2, over_x)
    direct_3 = move(kept_3, straight(0))
    crossed_2 = move(crossed_2, finish)
    core_far_2 = move(far_2, over_core)

    is_far = vector >= 2
    theirs = jnp.where(number // both == side, 0, 2)
    inner = lax.rem(number, both)
    second = (inner >= first_cut).astype(jnp.int32)
    last = number >= 2 * both
    bank = jnp.where(is_far, 5 * vector - 8 + jnp.where(last, 4, theirs + second), vector)
    place = jnp.where(
        is_far, jnp.where(last, number - 2 * both, inner - second * first_cut), low * across + high
    )
    table, starts = table_of(*jnp.broadcast_arrays(bank, place))
    choices = ((0,), (1,), (2, 3, 4, 5, 6), (7, 8, 9, 10, 11))
    banks = [cholesky, core_near]

    def part(which, vectors, total, added):
        pieces = [inputs[n] for n in which]
        first = pieces[0][0]
        return ladder_part(
            amplitudes, tiles, [piece[1:] for piece in pieces], banks, choices[:vectors], table,
            (first, len(choices), *starts), total, 2, added,
        )

    inputs = {
        "straight 1": (0, [(direct_1, 0), (kept_1, 0)], 2),
        "straight 2": (2, [(direct_2, 0), (kept_2, 0)], 1),
        "straight 3": (4, [(direct_3, 0), (kept_3, 0)], 1),
        "hop 1": (3, [(crossed_1, 0), (local, 0)], 1),
        "hop 2": (5, [(crossed_2, 0), (local, 1)], 1),
    }
    total = part(["straight 1", "straight 2", "hop 1"], 2, None, 0)
    side_1, side_2, far_3, direct_4, crossed_3 = gate(
        (side_1, side_2, far_3, direct_4, hops[2]),
        (direct_3, crossed_2, core_far_2, total),
    )
    core_far_3 = move(far_3, over_core)
    core_side_1, core_side_2 = move(side_1, over_core), move(side_2, over_core)
    direct_4 = move(direct_4, straight(1))
    crossed_3 = move(crossed_3, finish)
    inputs["straight 4"] = (6, [(direct_4, 0)], 1)
    inputs["hop 3"] = (7, [(crossed_3, 0), (local, 2)], 1)
    banks += [far_1, far_2, side_1, side_2, far_3]
    banks += [core_far_1, core_far_2, core_side_1, core_side_2, core_far_3]
    total = part(["straight 1", "straight 2", "hop 1", "straight 3", "hop 2"], 4, total, 4)
    return part(["straight 4", "hop 3"], 4, total, 0)


def solution(mesh):
    return jax.shard_map(
        functools.partial(shards, mesh.shape["orow"], mesh.shape["ocol"]),
        mesh=mesh,
        in_specs=(
            P("orow", "ocol", None, None),
            P("orow", "ocol", None, None),
            P(),
            P("ocol", None, None),
        ),
        out_specs=P("orow", "ocol", None, None),
        check_vma=False,
    )
```

```python
import functools

import jax
import jax.numpy as jnp
from jax import lax
from jax.experimental import pallas as pl
from jax.experimental.pallas import tpu as pltpu
from jax.sharding import PartitionSpec as P

AXES = ("orow", "ocol")
ANY = pl.BlockSpec(memory_space=pl.ANY)
VMEM = 56 * 2**20
DEEP = 2


def pack_kernel(sizes, width, place_ref, source_ref, *refs):
    held, sems = refs[-2:]
    packed = refs[-2 - len(sizes) : -2]
    loads, stores = [], []
    for part, size in enumerate(sizes):
        for inside in range(size):
            n = len(loads)
            row = pl.multiple_of(place_ref[3 * n + 1] * width, width)
            col = pl.multiple_of(place_ref[3 * n + 2] * width, width)
            loads.append(
                pltpu.make_async_copy(
                    source_ref.at[place_ref[3 * n], pl.ds(row, width), pl.ds(col, width)],
                    held.at[n],
                    sems.at[0, n],
                )
            )
            stores.append(pltpu.make_async_copy(held.at[n], packed[part].at[inside], sems.at[1, n]))
    for load in loads:
        load.start()
    for load, store in zip(loads, stores):
        load.wait()
        store.start()
    for store in stores:
        store.wait()


def pack(places, cholesky, width, sizes, after=()):
    count, dtype = sum(sizes), cholesky.dtype
    return pl.pallas_call(
        functools.partial(pack_kernel, sizes, width),
        out_shape=[jax.ShapeDtypeStruct((size, width, width), dtype) for size in sizes],
        grid_spec=pltpu.PrefetchScalarGridSpec(
            num_scalar_prefetch=1,
            grid=(1,),
            in_specs=[ANY] * (1 + len(after)),
            out_specs=[ANY] * len(sizes),
            scratch_shapes=[
                pltpu.VMEM((count, width, width), dtype),
                pltpu.SemaphoreType.DMA((2, count)),
            ],
        ),
        compiler_params=pltpu.CompilerParams(vmem_limit_bytes=VMEM),
        cost_estimate=pl.CostEstimate(
            flops=0, bytes_accessed=count * width * width // 16, transcendentals=0
        ),
        name="pack_tiles",
    )(places.reshape(-1), cholesky, *after)


def keep_tiles(source, mask_ref, base, tiles, width, store):
    for a in range(tiles):
        for b in range(tiles):
            rows, cols = slice(a * width, (a + 1) * width), slice(b * width, (b + 1) * width)
            block = source[rows, cols]
            store(rows, cols, block * mask_ref[base + a * tiles + b].astype(block.dtype))


def send_kernel(tiles, width, rows, col_pairs, first, *refs):
    start_ref, mask_ref, amps_ref = refs[:3]
    out_ref = refs[-1]
    pair = first + pl.program_id(0)
    base = ((pair // rows) * col_pairs + start_ref[0] + lax.rem(pair, rows)) * tiles * tiles

    def store(rows, cols, value):
        out_ref[0, rows, cols] = value

    keep_tiles(amps_ref.at[0, 0], mask_ref, base, tiles, width, store)


def sent_pairs(amplitudes, tile_mask, col, first, count, after=()):
    rows, col_pairs, depth, _ = amplitudes.shape
    tiles = tile_mask.shape[-1]

    def source(i, start, mask):
        return (first + i) // rows, start[0] + lax.rem(first + i, rows), 0, 0

    return pl.pallas_call(
        functools.partial(send_kernel, tiles, depth // tiles, rows, col_pairs, first),
        out_shape=jax.ShapeDtypeStruct((count, depth, depth), amplitudes.dtype),
        grid_spec=pltpu.PrefetchScalarGridSpec(
            num_scalar_prefetch=2,
            grid=(count,),
            in_specs=[pl.BlockSpec((1, 1, depth, depth), source)] + [ANY] * len(after),
            out_specs=pl.BlockSpec((1, depth, depth), lambda i, start, mask: (i, 0, 0)),
        ),
        compiler_params=pltpu.CompilerParams(vmem_limit_bytes=VMEM),
        cost_estimate=pl.CostEstimate(
            flops=0, bytes_accessed=count * depth * depth // 16, transcendentals=0
        ),
        name="sent_pairs",
    )(col.reshape(1).astype(jnp.int32), tile_mask.reshape(-1), amplitudes, *after)


class View:
    def __init__(self, ref, start):
        self.ref, self.start = ref, start

    def __getitem__(self, index):
        return self.ref[self.start + index]


def ladder_kernel(tiles, width, counts, number, choices, early, added, col_pairs, starts, *refs):
    table_ref, amps_ref = refs[:2]
    base_pair, stride = starts[:2]
    slots = [(a, b) for a in range(tiles) for b in range(a, tiles)]
    bank_ref, place_ref = (View(table_ref, start + base_pair * stride * len(slots)) for start in starts[2:4])
    flip_ref = View(table_ref, starts[4] + base_pair * len(slots))
    own_ref, mask_ref = View(table_ref, starts[5] + 3 * base_pair), View(table_ref, starts[6])
    pieces, at = [], 2
    for firsts, pairs in counts:
        pieces.append((refs[at : at + len(firsts)], firsts, pairs))
        at += len(firsts)
    banks = refs[at : at + number]
    total_ref = refs[at + number] if added else None
    out_ref, factor, weighted, partner, mine, sums, sems, block_sems = refs[-8:]
    pair, steps = pl.program_id(0), pl.num_programs(0)
    vectors = len(choices)

    def corner(index):
        return pl.ds(pl.multiple_of(index * width, width), width)

    def tile_of(bank, place):
        if bank.shape[-1] == width:
            return bank.at[place]
        across = bank.shape[-1] // width
        return bank.at[0, corner(place // across), corner(lax.rem(place, across))]

    def ends(which, pair):
        a, b = slots[which]
        if a == b:
            return a, b
        flip = flip_ref[pair * len(slots) + which]
        return a + flip * (b - a), b + flip * (a - b)

    def fetch(pair, slot, chosen):
        for vector in chosen:
            for which in range(len(slots)):
                entry = (pair * stride + vector) * len(slots) + which
                row, col = ends(which, pair)

                def begin(n):
                    pltpu.make_async_copy(
                        tile_of(banks[n], place_ref[entry]),
                        factor.at[slot, vector, corner(row), corner(col)],
                        sems.at[slot, vector, which],
                    ).start()

                if len(choices[vector]) == 1:
                    begin(choices[vector][0])
                else:
                    for n in choices[vector]:
                        pl.when(bank_ref[entry] == n)(functools.partial(begin, n))

    def fetch_partner(pair, slot):
        first = 0
        for arrays, firsts, pairs in pieces:
            for m, (array, start) in enumerate(zip(arrays, firsts)):
                here = (pair >= first) & (pair < first + pairs)
                if len(arrays) > 1:
                    here &= own_ref[3 * pair + 2] == m

                @pl.when(here)
                def _():
                    pltpu.make_async_copy(
                        array.at[start + pair - first], partner.at[slot], block_sems.at[slot, 0]
                    ).start()
            first += pairs

    def fetch_all(pair, slot):
        row, col = own_ref[3 * pair], own_ref[3 * pair + 1]
        pltpu.make_async_copy(amps_ref.at[row, col], mine.at[slot], block_sems.at[slot, 1]).start()
        fetch_partner(pair, slot)
        if added:
            pl.when(pair >= added)(lambda: fetch(pair, slot, range(early)))
        fetch(pair, slot, range(early if added else 0, vectors))
        if added:
            @pl.when(pair < added)
            def _():
                pltpu.make_async_copy(
                    total_ref.at[row, col], sums.at[slot], block_sems.at[slot, 2]
                ).start()

    slot = lax.rem(pair, DEEP)

    @pl.when(pair == 0)
    def _():
        fetch_all(pair, slot)

    def fetch_next():
        @pl.when(pair + 1 < steps)
        def _():
            fetch_all(pair + 1, 1 - slot)

    def store(rows, cols, value):
        weighted[rows, cols] = value

    base = (own_ref[3 * pair] * col_pairs + own_ref[3 * pair + 1]) * tiles * tiles
    pltpu.make_async_copy(amps_ref.at[0, 0], mine.at[slot], block_sems.at[slot, 1]).wait()
    keep_tiles(mine.at[slot], mask_ref, base, tiles, width, store)
    pltpu.make_async_copy(
        pieces[0][0][0].at[0], partner.at[slot], block_sems.at[slot, 0]
    ).wait()

    def arrive(chosen):
        for vector in chosen:
            for which in range(len(slots)):
                row, col = ends(which, pair)
                pltpu.make_async_copy(
                    tile_of(banks[0], 0),
                    factor.at[slot, vector, corner(row), corner(col)],
                    sems.at[slot, vector, which],
                ).wait()
                if slots[which][0] != slots[which][1]:
                    factor[slot, vector, corner(col), corner(row)] = factor[
                        slot, vector, corner(row), corner(col)
                    ].T

    def products(chosen):
        total = None
        for vector in chosen:
            whole = factor[slot, vector]
            inner = jnp.dot(whole, weighted[...], preferred_element_type=jnp.float32)
            inner += lax.dot_general(
                whole, partner[slot], (((1,), (1,)), ((), ())), preferred_element_type=jnp.float32
            )
            term = jnp.dot(inner.astype(jnp.bfloat16), whole, preferred_element_type=jnp.float32)
            total = term if total is None else total + term
        return total

    if not added:
        arrive(range(vectors))
        fetch_next()
        out_ref[0, 0] = products(range(vectors))
        return

    @pl.when(pair < added)
    def _():
        arrive(range(early, vectors))
        fetch_next()
        pltpu.make_async_copy(total_ref.at[0, 0], sums.at[slot], block_sems.at[slot, 2]).wait()
        out_ref[0, 0] = sums[slot] + products(range(early, vectors))

    @pl.when(pair >= added)
    def _():
        arrive(range(vectors))
        fetch_next()
        out_ref[0, 0] = products(range(vectors))


def ladder_part(amplitudes, tiles, pieces, banks, choices, table, starts, total, early, added):
    pairs, vectors = sum(count for _, count in pieces), len(choices)
    slots = tiles * (tiles + 1) // 2
    col_pairs, depth = amplitudes.shape[1:3]
    width = depth // tiles
    block = (1, 1, depth, depth)

    def own_map(pair, table):
        own = starts[5] + 3 * (starts[0] + pair)
        return table[own], table[own + 1], 0, 0

    in_specs, operands, counts = [ANY], [amplitudes], []
    for arrays, count in pieces:
        for array, _ in arrays:
            in_specs.append(ANY)
            operands.append(array)
        counts.append((tuple(start for _, start in arrays), count))
    in_specs += [ANY] * len(banks)
    operands += banks
    aliases = {}
    if total is not None:
        aliases = {1 + len(operands): 0}
        operands.append(total)
        in_specs.append(ANY)
    flops = 6 * pairs * vectors * depth**3
    moved = pairs * (depth * depth * 8 + vectors * slots * width * width * 2)
    return pl.pallas_call(
        functools.partial(
            ladder_kernel, tiles, width, tuple(counts), len(banks), choices, early, added, col_pairs,
            starts,
        ),
        out_shape=jax.ShapeDtypeStruct(amplitudes.shape, jnp.float32),
        grid_spec=pltpu.PrefetchScalarGridSpec(
            num_scalar_prefetch=1,
            grid=(pairs,),
            in_specs=in_specs,
            out_specs=pl.BlockSpec(block, own_map),
            scratch_shapes=[
                pltpu.VMEM((DEEP, vectors, depth, depth), jnp.bfloat16),
                pltpu.VMEM((depth, depth), jnp.bfloat16),
                pltpu.VMEM((DEEP, depth, depth), jnp.bfloat16),
                pltpu.VMEM((DEEP, depth, depth), jnp.bfloat16),
                pltpu.VMEM((DEEP if added else 1, depth, depth), jnp.float32),
                pltpu.SemaphoreType.DMA((DEEP, vectors, slots)),
                pltpu.SemaphoreType.DMA((DEEP, 3)),
            ],
        ),
        input_output_aliases=aliases,
        compiler_params=pltpu.CompilerParams(
            dimension_semantics=("arbitrary",), vmem_limit_bytes=VMEM
        ),
        cost_estimate=pl.CostEstimate(flops=flops // 64, bytes_accessed=moved // 64, transcendentals=0),
        name="ladder_part",
    )(table, *operands)


def gate_kernel(*refs):
    pass


def gate(values, after):
    return pl.pallas_call(
        gate_kernel,
        out_shape=[jax.ShapeDtypeStruct(value.shape, value.dtype) for value in values],
        in_specs=[ANY] * (len(values) + len(after)),
        out_specs=[ANY] * len(values),
        input_output_aliases={n: n for n in range(len(values))},
        compiler_params=pltpu.CompilerParams(vmem_limit_bytes=VMEM),
        cost_estimate=pl.CostEstimate(flops=0, bytes_accessed=0, transcendentals=0),
        name="gate",
    )(*values, *after)


def moves(rows, cols, change, chosen=lambda r, c: True):
    pairs = []
    for r in range(rows):
        for c in range(cols):
            if chosen(r, c):
                to_row, to_col = change(r, c)
                pairs.append((r * cols + c, to_row * cols + to_col))
    return pairs


def shards(rows, cols, amplitudes, tile_mask, domain_tiles, cholesky):
    row_pairs, col_pairs, depth, _ = amplitudes.shape
    tiles = domain_tiles.shape[-1]
    width = depth // tiles
    held = cholesky.shape[0]
    across = cholesky.shape[1] // width
    vectors = held * cols
    ratio = col_pairs // row_pairs
    r, c = lax.axis_index("orow"), lax.axis_index("ocol")

    paths = rows == 8 and cols == 4 and row_pairs == 2 and held == 1

    upper = [(s, t) for s in range(across) for t in range(s, across)]
    places = jnp.asarray([[q, s, t] for q in range(held) for s, t in upper], jnp.int32)
    first_cut, second_cut = len(upper) * 7 // 36, len(upper) * 7 // 36
    both = first_cut + second_cut

    order = (0, 1, 2, 5, 3, 6, 4, 7) if paths else tuple(range(row_pairs * col_pairs))
    pair = jnp.asarray(order, jnp.int32)
    turn = pair // (row_pairs * row_pairs)
    own_row = lax.rem(pair, row_pairs)
    own_col = lax.rem(r + ratio - turn, ratio) * row_pairs + lax.rem(pair // row_pairs, row_pairs)
    chosen = domain_tiles[r * row_pairs + own_row, c * col_pairs + own_col]
    corners = [(a, b) for a in range(tiles) for b in range(a, tiles)]
    first = jnp.stack([chosen[:, a] for a, _ in corners], axis=-1)
    second = jnp.stack([chosen[:, b] for _, b in corners], axis=-1)
    flip = (first > second).astype(jnp.int32)
    low, high = jnp.minimum(first, second), jnp.maximum(first, second)
    low, high = low[:, None, :], high[:, None, :]
    number = low * across - low * (low - 1) // 2 + high - low
    vector = jnp.arange(vectors, dtype=jnp.int32)[None, :, None]
    keeps = (c == r // ratio).astype(jnp.int32)
    at_home = (r // 4 == c // 2).astype(jnp.int32)
    source = jnp.where(turn == 0, keeps, jnp.where(pair == row_pairs**2, 0, at_home))
    source = jnp.where(paths, source, 0)
    own = jnp.stack([own_row, own_col, source], axis=-1)
    side = lax.rem(r, 2)

    def target(turn):
        return lambda a, b: (ratio * b + (a + turn) % ratio, a // ratio)

    def sent(turn, first, count, after=()):
        col = lax.rem(r + turn, ratio) * row_pairs
        return sent_pairs(amplitudes, tile_mask, col, first, count, after)

    def table_of(bank, place):
        parts = [jnp.ravel(part) for part in (bank, place, flip, own, tile_mask)]
        starts = [sum(part.size for part in parts[:n]) for n in range(len(parts))]
        return jnp.concatenate(parts).astype(jnp.int32), starts

    square = row_pairs * row_pairs
    if not paths:
        (packed,) = pack(places, cholesky, width, (len(places),))
        banks = [lax.all_gather(packed, "ocol", axis=0, tiled=True)]
        place = vector * len(upper) + number
        bank = jnp.zeros_like(place)
        pieces = [
            ([(lax.ppermute(sent(turn, 0, square), AXES, moves(rows, cols, target(turn))), 0)], square)
            for turn in range(ratio)
        ]
        table, starts = table_of(bank, place)
        choices = ((0,),) * vectors
        return ladder_part(
            amplitudes, tiles, pieces, banks, choices, table, (0, vectors, *starts), None, 0, 0
        )

    crosses = lambda a, b: (a // 4) != (b // 2)
    stays = lambda a, b: not crosses(a, b)
    over_y = moves(rows, cols, lambda a, b: (a, b ^ 2))
    over_x = moves(rows, cols, lambda a, b: (a ^ 1, b))
    over_core = moves(rows, cols, lambda a, b: (a, b ^ 1))
    hop = moves(rows, cols, lambda a, b: (a ^ 1, b ^ 2), crosses)

    finish = moves(rows, cols, lambda a, b: target(1)(a ^ 1, b ^ 2), stays)

    move = lambda value, pairs: lax.ppermute(value, AXES, pairs)
    straight = lambda turn: moves(rows, cols, target(turn), lambda a, b: target(turn)(a, b) != (a, b))
    stay = moves(rows, cols, target(1), stays)
    spot = side * both + jnp.arange(both, dtype=jnp.int32)

    core_near = move(cholesky, over_core)
    other = sent(1, 1, 3)
    hop_all = move(other, hop)
    far_1, far_2, far_3 = pack(
        jnp.concatenate([places[spot], places[2 * both :]]), cholesky, width,
        (first_cut, second_cut, len(upper) - 2 * both), (other,),
    )
    far_1 = move(far_1, over_y)
    kept_1 = sent(0, 0, 2, (other,))
    direct_1 = move(kept_1, straight(0))
    local = move(other, stay)
    kept_2, kept_3, direct_4 = sent(0, 2, 1, (other,)), sent(0, 3, 1, (other,)), sent(1, 0, 1, (other,))
    far_1, far_2, kept_2, kept_3, direct_4 = gate(
        (far_1, far_2, kept_2, kept_3, direct_4), (direct_1, core_near)
    )
    far_2 = move(far_2, over_y)
    side_1 = move(far_1, over_x)
    direct_2 = move(kept_2, straight(0))
    hops = [hop_all[n : n + 1] for n in range(3)]
    crossed_1 = move(hops[0], finish)
    core_far_1 = move(far_1, over_core)
    far_2, far_3, kept_3, crossed_2 = gate(
        (far_2, far_3, kept_3, hops[1]),
        (side_1, direct_2, crossed_1, core_far_1, local),
    )
    far_3 = move(far_3, over_y)
    side_2 = move(far_2, over_x)
    direct_3 = move(kept_3, straight(0))
    crossed_2 = move(crossed_2, finish)
    core_far_2 = move(far_2, over_core)

    is_far = vector >= 2
    theirs = jnp.where(number // both == side, 0, 2)
    inner = lax.rem(number, both)
    second = (inner >= first_cut).astype(jnp.int32)
    last = number >= 2 * both
    bank = jnp.where(is_far, 5 * vector - 8 + jnp.where(last, 4, theirs + second), vector)
    place = jnp.where(
        is_far, jnp.where(last, number - 2 * both, inner - second * first_cut), low * across + high
    )
    table, starts = table_of(*jnp.broadcast_arrays(bank, place))
    choices = ((0,), (1,), (2, 3, 4, 5, 6), (7, 8, 9, 10, 11))
    banks = [cholesky, core_near]

    def part(which, vectors, total, added):
        pieces = [inputs[n] for n in which]
        first = pieces[0][0]
        return ladder_part(
            amplitudes, tiles, [piece[1:] for piece in pieces], banks, choices[:vectors], table,
            (first, len(choices), *starts), total, 2, added,
        )

    inputs = {
        "straight 1": (0, [(direct_1, 0), (kept_1, 0)], 2),
        "straight 2": (2, [(direct_2, 0), (kept_2, 0)], 1),
        "straight 3": (4, [(direct_3, 0), (kept_3, 0)], 1),
        "hop 1": (3, [(crossed_1, 0), (local, 0)], 1),
        "hop 2": (5, [(crossed_2, 0), (local, 1)], 1),
    }
    total = part(["straight 1", "straight 2", "hop 1"], 2, None, 0)
    side_1, side_2, far_3, direct_4, crossed_3 = gate(
        (side_1, side_2, far_3, direct_4, hops[2]),
        (direct_3, crossed_2, core_far_2, total),
    )
    core_far_3 = move(far_3, over_core)
    core_side_1, core_side_2 = move(side_1, over_core), move(side_2, over_core)
    direct_4 = move(direct_4, straight(1))
    crossed_3 = move(crossed_3, finish)
    inputs["straight 4"] = (6, [(direct_4, 0)], 1)
    inputs["hop 3"] = (7, [(crossed_3, 0), (local, 2)], 1)
    banks += [far_1, far_2, side_1, side_2, far_3]
    banks += [core_far_1, core_far_2, core_side_1, core_side_2, core_far_3]
    total = part(["straight 1", "straight 2", "hop 1", "straight 3", "hop 2"], 4, total, 4)
    return part(["straight 4", "hop 3"], 4, total, 0)


def solution(mesh):
    return jax.shard_map(
        functools.partial(shards, mesh.shape["orow"], mesh.shape["ocol"]),
        mesh=mesh,
        in_specs=(
            P("orow", "ocol", None, None),
            P("orow", "ocol", None, None),
            P(),
            P("ocol", None, None),
        ),
        out_specs=P("orow", "ocol", None, None),
        check_vma=False,
    )
```
